32 devices in a mesh: grp: 4 (over y, x), in: 8 (over z, core).
Axes of the slice: x: 2, y: 2, z: 4, core: 2. Of those that a mesh axis runs over, the one named last changes fastest.
Arguments:
- unfolding: float32 [1024, 131072], P(None, ('grp', 'in')), may hold values from -300 to 300
- start_basis: float32 [1024, 128], replicated, may hold values from -6 to 6
Outputs:
- factor: float32 [1024, 128], replicated
- core_block: float32 [128, 131072], P(None, ('grp', 'in'))
The draws below stay inside these ranges and needn't reach their ends.
All inputs are finite; a program needn't handle non-finite values.
Results may differ from the reference program's by a relative error of at most 0.0003.
Values sent between devices are 32-bit elements; how exact they have to be, the bound alone decides.
No kernel may reach another device: no remote copies, remote signals or barrier semaphores. Data moves between devices by JAX's collectives and lax.ppermute only.
A program may use at most 128 MiB of HBM per device.

```python
import jax
import jax.numpy as jnp
from jax import lax

I1 = 1024
RANK = 128
ITERS = 3
COLS = 131072


def draw_unfolding(key, part):
    key_rows, key_cols, key_left, key_right, key_noise = jax.random.split(key, 5)
    row_scale = jnp.exp(jax.random.uniform(key_rows, (I1, 1), jnp.float32, 0.0, jnp.log(10.0)))
    ramp = 1.0 + 2.0 * jnp.arange(COLS, dtype=jnp.float32) / COLS
    col_scale = jnp.exp(jax.random.uniform(key_cols, (1, COLS), jnp.float32, 0.0, jnp.log(2.0))) * ramp[None, :]
    decay = jnp.exp(-2.0 * jnp.arange(RANK, dtype=jnp.float32) / RANK)
    left = jnp.clip(jax.random.normal(key_left, (I1, RANK), jnp.float32), -5.0, 5.0)
    right = jnp.clip(jax.random.normal(key_right, (COLS, RANK), jnp.float32), -5.0, 5.0)
    noise = 0.1 * jnp.clip(jax.random.normal(key_noise, (I1, COLS), jnp.float32), -5.0, 5.0)
    signal = jnp.dot(left * decay[None, :], right.T, precision=lax.Precision.HIGHEST, preferred_element_type=jnp.float32) / jnp.sqrt(jnp.float32(RANK))
    return jnp.clip(row_scale * col_scale * (signal + noise), -300.0, 300.0).astype(jnp.float32)


def centred(rng, extent, width, reach, held_as=jnp.bfloat16):
    result = jax.random.normal(rng, extent, jnp.float32) * width
    return jnp.minimum(jnp.maximum(result, -reach), reach).astype(held_as)


def setup_inputs(seed: int = 0) -> dict:
    splits = jax.random.split(jax.random.key(seed), 3)
    unfolding = draw_unfolding(jax.random.fold_in(splits[2], 71), 0)
    start_basis = centred(splits[1], (I1, RANK), 1.0, 6.0, jnp.float32)
    return {"unfolding": unfolding, "start_basis": start_basis}


def orthonormal(image):
    inner = jnp.dot(image.T.astype(jnp.float32), image.astype(jnp.float32), precision=lax.Precision.HIGHEST, preferred_element_type=jnp.float32)
    lower = jnp.linalg.cholesky(inner)
    return lax.linalg.triangular_solve(lower, image, left_side=False, lower=True, transpose_a=True)

def reference(unfolding, start_basis):
    gram = lax.dot_general(unfolding.astype(jnp.float32), unfolding.astype(jnp.float32), (((1,), (1,)), ((), ())), precision=lax.Precision.HIGHEST, preferred_element_type=jnp.float32)
    basis = start_basis
    for step in range(ITERS):
        image = jnp.dot(gram.astype(jnp.float32), basis.astype(jnp.float32), precision=lax.Precision.HIGHEST, preferred_element_type=jnp.float32)
        basis = orthonormal(image)
    core_block = jnp.dot(basis.T.astype(jnp.float32), unfolding.astype(jnp.float32), precision=lax.Precision.HIGHEST, preferred_element_type=jnp.float32)
    return (basis, core_block)
```

```python
import functools

import jax
import jax.numpy as jnp
from jax import lax
from jax.experimental import pallas as pl
from jax.experimental.pallas import tpu as pltpu
from jax.sharding import PartitionSpec as P

ITERS = 3
BLOCKS = 4
F32 = jnp.float32
BF16 = jnp.bfloat16
NT = (((1,), (1,)), ((), ()))
NN = (((1,), (0,)), ((), ()))
VMEM_LIMIT = 56 * 1024 * 1024

CHUNKS = (
    (((0, 0), (0, 1)), ((1, 1), (1, 2))),
    (((0, 2), (0, 3), (3, 3)), ((1, 3), (2, 2), (2, 3))),
)


def split(value):
    high = value.astype(BF16)
    low = (value - high.astype(F32)).astype(BF16)
    return high, low


def mm(left, right, dims):
    return lax.dot_general(left, right, dims, preferred_element_type=F32)


def gram_kernel(chunk, bs, u_ref, out_ref, high_ref, low_ref, cross_ref):
    step = pl.program_id(0)
    rows = u_ref.shape[0]
    for lo in range(0, rows, bs):
        high, low = split(u_ref[lo : lo + bs, :])
        high_ref[lo : lo + bs, :] = high
        low_ref[lo : lo + bs, :] = low

    @pl.when(step == 0)
    def _():
        out_ref[...] = jnp.zeros_like(out_ref)
        cross_ref[...] = jnp.zeros_like(cross_ref)

    def part(ref, i):
        return ref[i * bs : (i + 1) * bs, :]

    diagonal = 0
    for core, blocks in enumerate(chunk):
        for place, (i, j) in enumerate(blocks):
            cols = slice(place * bs, (place + 1) * bs)
            hi = part(high_ref, i)
            if i == j:
                out_ref[core, :, cols] += mm(hi, hi, NT)
                cross_ref[diagonal] += mm(hi, part(low_ref, i), NT)
                diagonal += 1
            else:
                hj = part(high_ref, j)
                out_ref[core, :, cols] += (
                    mm(hi, hj, NT) + mm(hi, part(low_ref, j), NT) + mm(part(low_ref, i), hj, NT)
                )

    @pl.when(step == pl.num_programs(0) - 1)
    def _():
        diagonal = 0
        for core, blocks in enumerate(chunk):
            for place, (i, j) in enumerate(blocks):
                if i == j:
                    cols = slice(place * bs, (place + 1) * bs)
                    cross = cross_ref[diagonal]
                    out_ref[core, :, cols] += cross + cross.T
                    diagonal += 1


def gram_chunk(unfolding, chunk):
    order, depth = unfolding.shape
    bs = order // BLOCKS
    used = (1 + max(j for blocks in chunk for _, j in blocks)) * bs
    width = len(chunk[0]) * bs
    diagonals = sum(i == j for blocks in chunk for i, j in blocks)
    step = min(512, depth)
    return pl.pallas_call(
        functools.partial(gram_kernel, chunk, bs),
        grid=(depth // step,),
        in_specs=[pl.BlockSpec((used, step), lambda k: (0, k))],
        out_specs=pl.BlockSpec((2, bs, width), lambda k: (0, 0, 0)),
        out_shape=jax.ShapeDtypeStruct((2, bs, width), F32),
        scratch_shapes=[
            pltpu.VMEM((used, step), BF16),
            pltpu.VMEM((used, step), BF16),
            pltpu.VMEM((diagonals, bs, bs), F32),
        ],
        compiler_params=pltpu.CompilerParams(vmem_limit_bytes=VMEM_LIMIT),
        name="gram",
    )(unfolding)


def split_kernel(u_ref, high_ref, low_ref):
    high, low = split(u_ref[...])
    high_ref[...] = high
    low_ref[...] = low


def split_columns(unfolding):
    order, depth = unfolding.shape
    step = order // 8
    spec = pl.BlockSpec((step, depth), lambda k: (k, 0))
    return pl.pallas_call(
        split_kernel,
        grid=(order // step,),
        in_specs=[spec],
        out_specs=[spec, spec],
        out_shape=[jax.ShapeDtypeStruct((order, depth), BF16)] * 2,
        compiler_params=pltpu.CompilerParams(vmem_limit_bytes=VMEM_LIMIT),
        name="split",
    )(unfolding)


def inverse_cholesky(inner):
    order = inner.shape[0]
    groups = order // 8
    shape = (8, order)
    lane = lax.broadcasted_iota(jnp.int32, shape, 1)
    sub = lax.broadcasted_iota(jnp.int32, shape, 0)

    def lanes(value, k):
        return jnp.broadcast_to(value[:, k : k + 1], shape)

    def subs(value, i):
        return jnp.broadcast_to(value[i : i + 1, :], shape)

    rows = [inner[8 * m : 8 * m + 8, :] for m in range(groups)]
    result = []
    for b in range(groups):
        first = 8 * b
        inside = (lane >= first) & (lane < first + 8)
        own = rows[b]
        column = [lanes(own, first + k) for k in range(8)]
        s = [[subs(column[k], i) for k in range(i + 1)] for i in range(8)]
        masked = jnp.where(inside, jnp.where(lane == first + sub, 1.0, 0.0), own)
        y = [subs(masked, i) for i in range(8)]
        inverse = [None] * 8
        f = [[None] * 8 for _ in range(8)]
        for k in range(8):
            inverse[k] = 1.0 / s[k][k]
            for i in range(k + 1, 8):
                f[i][k] = s[i][k] * inverse[k]
            for i in range(k + 1, 8):
                for j in range(k + 1, i + 1):
                    s[i][j] = s[i][j] - f[i][k] * s[j][k]
                y[i] = y[i] - f[i][k] * y[k]
        p = [y[k] * inverse[k] for k in range(8)]
        for i in range(6, -1, -1):
            for j in range(i + 1, 8):
                p[i] = p[i] - f[j][i] * p[j]
        out = y[0] * lax.rsqrt(s[0][0])
        for i in range(1, 8):
            out = jnp.where(sub == i, y[i] * lax.rsqrt(s[i][i]), out)
        result.append(jnp.where(lane <= first + sub, out, 0.0))
        for m in range(b + 1, groups):
            value = jnp.where(inside, 0.0, rows[m])
            for k in range(8):
                value = value - lanes(rows[m], first + k) * p[k]
            rows[m] = value
    return jnp.concatenate(result, axis=0)


def mm6(left, right, dims):
    return lax.dot_general(
        left, right, dims, precision=lax.Precision.HIGHEST, preferred_element_type=F32
    )


def iterate_kernel(
    bs, widths, start_ref, *refs
):
    chunk_refs = refs[: len(CHUNKS)]
    high_hbm, low_hbm, factor_ref, core_ref = refs[len(CHUNKS) : len(CHUNKS) + 4]
    g_high, g_low, basis, image, u_high, u_low, sems = refs[len(CHUNKS) + 4 :]
    rank = start_ref.shape[0]
    copies = (
        pltpu.make_async_copy(high_hbm, u_high, sems.at[0]),
        pltpu.make_async_copy(low_hbm, u_low, sems.at[1]),
    )
    for copy in copies:
        copy.start()
    slot = {}
    for ref, chunk in zip(chunk_refs, CHUNKS):
        for core, blocks in enumerate(chunk):
            for place, pair in enumerate(blocks):
                number = len(slot)
                slot[pair] = number
                high, low = split(ref[core, :, place * bs : (place + 1) * bs])
                g_high[number] = high
                g_low[number] = low
    basis[...] = start_ref[...]

    def body(_, carry):
        high, low = split(basis[...])
        both = jnp.concatenate([high, low], axis=0)
        for j in range(BLOCKS):
            total = None
            extra = None
            for i in range(BLOCKS):
                pair, dims = ((i, j), NN) if i <= j else ((j, i), NT)
                cols = slice(i * bs, (i + 1) * bs)
                t = mm(both[:, cols], g_high[slot[pair]], dims)
                e = mm(high[:, cols], g_low[slot[pair]], dims)
                total = t if total is None else total + t
                extra = e if extra is None else extra + e
            image[:, j * bs : (j + 1) * bs] = total[:rank] + (total[rank:] + extra)
        inner = mm6(image[...], image[...], NT)
        basis[...] = mm6(inverse_cholesky(inner), image[...], NN)
        return carry

    lax.fori_loop(0, ITERS, body, 0)
    factor_ref[...] = basis[...].T
    for copy in copies:
        copy.wait()
    high, low = split(basis[...])
    both = jnp.concatenate([high, low], axis=0)
    depth = u_high.shape[1]
    step = min(512, depth)
    for lo in range(0, depth, step):
        cols = slice(lo, lo + step)
        total = mm(both, u_high[:, cols], NN)
        core_ref[:, cols] = total[:rank] + (total[rank:] + mm(high, u_low[:, cols], NN))


def iterate(start, chunks, high, low):
    rank, order = start.shape
    depth = high.shape[1]
    bs = order // BLOCKS
    count = sum(len(blocks) for chunk in CHUNKS for blocks in chunk)
    vmem = pl.BlockSpec(memory_space=pltpu.VMEM)
    hbm = pl.BlockSpec(memory_space=pl.ANY)
    return pl.pallas_call(
        functools.partial(iterate_kernel, bs, None),
        in_specs=[vmem] * (1 + len(chunks)) + [hbm] * 2,
        out_specs=[vmem, vmem],
        out_shape=[
            jax.ShapeDtypeStruct((order, rank), F32),
            jax.ShapeDtypeStruct((rank, depth), F32),
        ],
        scratch_shapes=[
            pltpu.VMEM((count, bs, bs), BF16),
            pltpu.VMEM((count, bs, bs), BF16),
            pltpu.VMEM((rank, order), F32),
            pltpu.VMEM((rank, order), F32),
            pltpu.VMEM((order, depth), BF16),
            pltpu.VMEM((order, depth), BF16),
            pltpu.SemaphoreType.DMA((2,)),
        ],
        compiler_params=pltpu.CompilerParams(vmem_limit_bytes=VMEM_LIMIT),
        name="iterate",
    )(start, *chunks, high, low)


def swap(value, axis, size, bits):
    return lax.ppermute(value, axis, [(i, i ^ bits) for i in range(size)])


def scatter_sum(value, axis, size, shift, count, place):
    total = lax.dynamic_index_in_dim(value, place, 0, keepdims=False)
    for r in range(1, count):
        part = lax.dynamic_index_in_dim(value, place ^ r, 0, keepdims=False)
        total = total + swap(part, axis, size, r << shift)
    return total


def gather(value, axis, size, shift, count, place):
    whole = jnp.zeros((count,) + value.shape, value.dtype)
    whole = lax.dynamic_update_index_in_dim(whole, value, place, 0)
    for r in range(1, count):
        part = swap(value, axis, size, r << shift)
        whole = lax.dynamic_update_index_in_dim(whole, part, place ^ r, 0)
    return whole


def all_sum(value, groups, inner):
    g = lax.axis_index("grp")
    i = lax.axis_index("in")
    core, z = i & 1, i >> 1
    nz = inner // 2
    _, bs, width = value.shape
    half = scatter_sum(value, "in", inner, 0, 2, core)
    quarter = scatter_sum(half.reshape(groups, bs // groups, width), "grp", groups, 0, groups, g)
    piece = scatter_sum(quarter.reshape(nz, bs // groups // nz, width), "in", inner, 1, nz, z)
    quarter = gather(piece, "in", inner, 1, nz, z).reshape(bs // groups, width)
    half = gather(quarter, "grp", groups, 0, groups, g).reshape(bs, width)
    return gather(half, "in", inner, 0, 2, core)


def per_device(groups, inner, unfolding, start_basis):
    chunks = [all_sum(gram_chunk(unfolding, chunk), groups, inner) for chunk in CHUNKS]
    high, low = split_columns(unfolding)
    factor, core_block = iterate(start_basis.T, chunks, high, low)
    return (factor, core_block)


def solution(mesh):
    in_specs = (P(None, ("grp", "in")), P())
    out_specs = (P(), P(None, ("grp", "in")))
    body = functools.partial(per_device, mesh.shape["grp"], mesh.shape["in"])
    return jax.shard_map(body, mesh=mesh, in_specs=in_specs, out_specs=out_specs, check_vma=False)
```

```python
import functools

import jax
import jax.numpy as jnp
from jax import lax
from jax.experimental import pallas as pl
from jax.experimental.pallas import tpu as pltpu
from jax.sharding import PartitionSpec as P

ITERS = 3
BLOCKS = 4
F32 = jnp.float32
BF16 = jnp.bfloat16
NT = (((1,), (1,)), ((), ()))
NN = (((1,), (0,)), ((), ()))
VMEM_LIMIT = 56 * 1024 * 1024

CHUNKS = ((2, 1), (3, 0))


def split(value):
    high = value.astype(BF16)
    low = (value - high.astype(F32)).astype(BF16)
    return high, low


def mm(left, right, dims):
    return lax.dot_general(left, right, dims, preferred_element_type=F32)


def gram_kernel(chunk, bs, u_ref, out_ref, high_ref, low_ref, cross_ref):
    step = pl.program_id(0)
    rows = u_ref.shape[0]
    for lo in range(0, rows, bs):
        high, low = split(u_ref[lo : lo + bs, :])
        high_ref[lo : lo + bs, :] = high
        low_ref[lo : lo + bs, :] = low

    @pl.when(step == 0)
    def _():
        out_ref[...] = jnp.zeros_like(out_ref)
        cross_ref[...] = jnp.zeros_like(cross_ref)

    base = 0
    for number, j in enumerate(chunk):
        above, end = j * bs, (j + 1) * bs
        hj = high_ref[above:end, :]
        lj = low_ref[above:end, :]
        out_ref[base : base + end, :] += mm(high_ref[:end, :], hj, NT)
        if j:
            out_ref[base : base + above, :] += mm(low_ref[:above, :], hj, NT)
        cross = mm(high_ref[:end, :], lj, NT)
        if j:
            out_ref[base : base + above, :] += cross[:above]
        cross_ref[number] += cross[above:]
        base += end

    @pl.when(step == pl.num_programs(0) - 1)
    def _():
        base = 0
        for number, j in enumerate(chunk):
            above, end = j * bs, (j + 1) * bs
            cross = cross_ref[number]
            out_ref[base + above : base + end, :] += cross + cross.T
            base += end


def gram_chunk(unfolding, chunk):
    order, depth = unfolding.shape
    bs = order // BLOCKS
    used = (1 + max(chunk)) * bs
    height = sum(1 + j for j in chunk) * bs
    step = min(512, depth)
    return pl.pallas_call(
        functools.partial(gram_kernel, chunk, bs),
        grid=(depth // step,),
        in_specs=[pl.BlockSpec((used, step), lambda k: (0, k))],
        out_specs=pl.BlockSpec((height, bs), lambda k: (0, 0)),
        out_shape=jax.ShapeDtypeStruct((height, bs), F32),
        scratch_shapes=[
            pltpu.VMEM((used, step), BF16),
            pltpu.VMEM((used, step), BF16),
            pltpu.VMEM((len(chunk), bs, bs), F32),
        ],
        compiler_params=pltpu.CompilerParams(vmem_limit_bytes=VMEM_LIMIT),
        name="gram",
    )(unfolding)


def inverse_cholesky(inner):
    order = inner.shape[0]
    groups = order // 8
    shape = (8, order)
    lane = lax.broadcasted_iota(jnp.int32, shape, 1)
    sub = lax.broadcasted_iota(jnp.int32, shape, 0)

    def lanes(value, k):
        return jnp.broadcast_to(value[:, k : k + 1], shape)

    def subs(value, i):
        return jnp.broadcast_to(value[i : i + 1, :], shape)

    rows = [inner[8 * m : 8 * m + 8, :] for m in range(groups)]
    result = []
    for b in range(groups):
        first = 8 * b
        inside = (lane >= first) & (lane < first + 8)
        own = rows[b]
        column = [lanes(own, first + k) for k in range(8)]
        s = [[subs(column[k], i) for k in range(i + 1)] for i in range(8)]
        masked = jnp.where(inside, jnp.where(lane == first + sub, 1.0, 0.0), own)
        y = [subs(masked, i) for i in range(8)]
        inverse = [None] * 8
        f = [[None] * 8 for _ in range(8)]
        for k in range(8):
            inverse[k] = 1.0 / s[k][k]
            for i in range(k + 1, 8):
                f[i][k] = s[i][k] * inverse[k]
            for i in range(k + 1, 8):
                for j in range(k + 1, i + 1):
                    s[i][j] = s[i][j] - f[i][k] * s[j][k]
                y[i] = y[i] - f[i][k] * y[k]
        p = [y[k] * inverse[k] for k in range(8)]
        for i in range(6, -1, -1):
            for j in range(i + 1, 8):
                p[i] = p[i] - f[j][i] * p[j]
        out = y[0] * lax.rsqrt(s[0][0])
        for i in range(1, 8):
            out = jnp.where(sub == i, y[i] * lax.rsqrt(s[i][i]), out)
        result.append(jnp.where(lane <= first + sub, out, 0.0))
        for m in range(b + 1, groups):
            value = jnp.where(inside, 0.0, rows[m])
            for k in range(8):
                value = value - lanes(rows[m], first + k) * p[k]
            rows[m] = value
    return jnp.concatenate(result, axis=0)


def mm6(left, right, dims):
    return lax.dot_general(
        left, right, dims, precision=lax.Precision.HIGHEST, preferred_element_type=F32
    )


def iterate_kernel(bs, start_ref, *refs):
    count = len(CHUNKS)
    chunk_refs = refs[:count]
    u_hbm, factor_ref, core_ref, g_high, g_low, basis, image, u_vmem, sem = refs[count:]
    rank = start_ref.shape[0]
    copy = pltpu.make_async_copy(u_hbm, u_vmem, sem)
    copy.start()
    slot = {}
    for ref, chunk in zip(chunk_refs, CHUNKS):
        base = 0
        for j in chunk:
            for i in range(j + 1):
                number = len(slot)
                slot[i, j] = number
                high, low = split(ref[base : base + bs, :])
                g_high[number] = high
                g_low[number] = low
                base += bs
    basis[...] = start_ref[...]

    def body(_, carry):
        high, low = split(basis[...])
        both = jnp.concatenate([high, low], axis=0)
        for j in range(BLOCKS):
            total = None
            extra = None
            for i in range(BLOCKS):
                pair, dims = ((i, j), NN) if i <= j else ((j, i), NT)
                cols = slice(i * bs, (i + 1) * bs)
                t = mm(both[:, cols], g_high[slot[pair]], dims)
                e = mm(high[:, cols], g_low[slot[pair]], dims)
                total = t if total is None else total + t
                extra = e if extra is None else extra + e
            image[:, j * bs : (j + 1) * bs] = total[:rank] + (total[rank:] + extra)
        inner = mm6(image[...], image[...], NT)
        basis[...] = mm6(inverse_cholesky(inner), image[...], NN)
        return carry

    lax.fori_loop(0, ITERS, body, 0)
    factor_ref[...] = basis[...].T
    copy.wait()
    high, low = split(basis[...])
    both = jnp.concatenate([high, low], axis=0)
    depth = u_vmem.shape[1]
    step = min(512, depth)
    for lo in range(0, depth, step):
        cols = slice(lo, lo + step)
        u_high, u_low = split(u_vmem[:, cols])
        total = mm(both, u_high, NN)
        core_ref[:, cols] = total[:rank] + (total[rank:] + mm(high, u_low, NN))


def iterate(start, chunks, unfolding):
    rank, order = start.shape
    depth = unfolding.shape[1]
    bs = order // BLOCKS
    count = sum(1 + j for chunk in CHUNKS for j in chunk)
    vmem = pl.BlockSpec(memory_space=pltpu.VMEM)
    hbm = pl.BlockSpec(memory_space=pl.ANY)
    return pl.pallas_call(
        functools.partial(iterate_kernel, bs),
        in_specs=[vmem] * (1 + len(chunks)) + [hbm],
        out_specs=[vmem, vmem],
        out_shape=[
            jax.ShapeDtypeStruct((order, rank), F32),
            jax.ShapeDtypeStruct((rank, depth), F32),
        ],
        scratch_shapes=[
            pltpu.VMEM((count, bs, bs), BF16),
            pltpu.VMEM((count, bs, bs), BF16),
            pltpu.VMEM((rank, order), F32),
            pltpu.VMEM((rank, order), F32),
            pltpu.VMEM((order, depth), F32),
            pltpu.SemaphoreType.DMA,
        ],
        compiler_params=pltpu.CompilerParams(vmem_limit_bytes=VMEM_LIMIT),
        name="iterate",
    )(start, *chunks, unfolding)


def pair_swap(value, size):
    return lax.ppermute(value, "in", [(i, i ^ 1) for i in range(size)])


def spread(value, count, axis, groups):
    parts = value.reshape((count, value.shape[0] // count) + value.shape[1:])
    return lax.all_to_all(parts, axis, 0, 0, axis_index_groups=groups)


def scatter_sum(value, count, axis, groups=None):
    return jnp.sum(spread(value, count, axis, groups), axis=0)


def gather(value, count, axis, groups=None):
    whole = jnp.broadcast_to(value[None], (count,) + value.shape)
    whole = lax.all_to_all(whole, axis, 0, 0, axis_index_groups=groups)
    return whole.reshape((-1,) + value.shape[1:])


def all_sum(value, groups, inner):
    core = lax.axis_index("in") & 1
    columns = [[2 * z + c for z in range(inner // 2)] for c in range(2)]
    height = value.shape[0] // 2
    sent = lax.dynamic_slice_in_dim(value, (1 - core) * height, height, 0)
    kept = lax.dynamic_slice_in_dim(value, core * height, height, 0)
    half = kept + pair_swap(sent, inner)
    quarter = scatter_sum(half, groups, "grp")
    piece = scatter_sum(quarter, inner // 2, "in", columns)
    quarter = gather(piece, inner // 2, "in", columns)
    half = gather(quarter, groups, "grp")
    other = pair_swap(half, inner)
    first = core == 0
    return jnp.concatenate([jnp.where(first, half, other), jnp.where(first, other, half)], axis=0)


def per_device(groups, inner, unfolding, start_basis):
    chunks = [all_sum(gram_chunk(unfolding, chunk), groups, inner) for chunk in CHUNKS]
    factor, core_block = iterate(start_basis.T, chunks, unfolding)
    return (factor, core_block)


def solution(mesh):
    in_specs = (P(None, ("grp", "in")), P())
    out_specs = (P(), P(None, ("grp", "in")))
    body = functools.partial(per_device, mesh.shape["grp"], mesh.shape["in"])
    return jax.shard_map(body, mesh=mesh, in_specs=in_specs, out_specs=out_specs, check_vma=False)
```

```python
import functools

import jax
import jax.numpy as jnp
from jax import lax
from jax.experimental import pallas as pl
from jax.experimental.pallas import tpu as pltpu
from jax.sharding import PartitionSpec as P

ITERS = 3
BLOCKS = 4
F32 = jnp.float32
BF16 = jnp.bfloat16
NT = (((1,), (1,)), ((), ()))
NN = (((1,), (0,)), ((), ()))
VMEM_LIMIT = 44 * 1024 * 1024

CHUNKS = ((3, 0), (2, 1))


def split(value):
    high = value.astype(BF16)
    low = (value - high.astype(F32)).astype(BF16)
    return high, low


def mm(left, right, dims):
    return lax.dot_general(left, right, dims, preferred_element_type=F32)


def units(chunk, bs):
    half = bs // 2
    for j in chunk:
        for i in range(j + 1):
            yield i, j, 0, (half if i == j else bs)
            yield i, j, 1, bs


def packed_rows(chunk, bs):
    return sum(rows for *_, rows in units(chunk, bs))


def gram_kernel(bs, u_ref, start_ref, *refs):
    outs = refs[: 2 * len(CHUNKS)]
    start_out, both_ref, acc_ref, cross_ref, packed_ref = refs[2 * len(CHUNKS) :]
    step = pl.program_id(0)
    rows, depth = u_ref.shape

    @pl.when(step == 0)
    def _():
        acc_ref[...] = jnp.zeros_like(acc_ref)
        cross_ref[...] = jnp.zeros_like(cross_ref)
        high, low = split(start_ref[...].T)
        start_out[: high.shape[0], :] = high
        start_out[high.shape[0] :, :] = low

    for lo in range(0, rows, bs):
        high, low = split(u_ref[lo : lo + bs, :])
        both_ref[lo : lo + bs, 0 * depth : 1 * depth] = high
        both_ref[lo : lo + bs, 1 * depth : 2 * depth] = high
        both_ref[lo : lo + bs, 2 * depth : 3 * depth] = low
        both_ref[lo : lo + bs, 3 * depth : 4 * depth] = high

    for j in range(BLOCKS):
        above, end = j * bs, (j + 1) * bs
        if j:
            acc_ref[:above, above:end] += mm(
                both_ref[:above, depth : 4 * depth], both_ref[above:end, : 3 * depth], NT
            )
        high = both_ref[above:end, :depth]
        acc_ref[above:end, above:end] += mm(high, high, NT)
        cross_ref[j] += mm(high, both_ref[above:end, 2 * depth : 3 * depth], NT)

    @pl.when(step == pl.num_programs(0) - 1)
    def _():
        core = lax.rem(lax.axis_index("in"), 2)
        for j in range(BLOCKS):
            above, end = j * bs, (j + 1) * bs
            acc_ref[above:end, above:end] += cross_ref[j] + cross_ref[j].T
        for number, chunk in enumerate(CHUNKS):
            base = 0
            for i, j, half, height in units(chunk, bs):
                left = j * bs + half * (bs // 2)
                packed_ref[number, base : base + height, :] = acc_ref[
                    i * bs : i * bs + height, left : left + bs // 2
                ]
                base += height
            sent, kept = outs[2 * number : 2 * number + 2]
            part = sent.shape[0]
            sent[...] = packed_ref[number, pl.ds(pl.multiple_of((1 - core) * part, part), part), :]
            kept[...] = packed_ref[number, pl.ds(pl.multiple_of(core * part, part), part), :]


def gram(unfolding, start):
    order, depth = unfolding.shape
    rank = start.shape[1]
    bs = order // BLOCKS
    height = packed_rows(CHUNKS[0], bs)
    step = min(1024, depth)
    part = jax.ShapeDtypeStruct((height // 2, bs // 2), F32)
    count = 2 * len(CHUNKS)
    return pl.pallas_call(
        functools.partial(gram_kernel, bs),
        grid=(depth // step,),
        in_specs=[
            pl.BlockSpec((order, step), lambda k: (0, k)),
            pl.BlockSpec((order, rank), lambda k: (0, 0)),
        ],
        out_specs=[pl.BlockSpec((height // 2, bs // 2), lambda k: (0, 0))] * count
        + [pl.BlockSpec((2 * rank, order), lambda k: (0, 0))],
        out_shape=[part] * count + [jax.ShapeDtypeStruct((2 * rank, order), BF16)],
        scratch_shapes=[
            pltpu.VMEM((order, 4 * step), BF16),
            pltpu.VMEM((order, order), F32),
            pltpu.VMEM((BLOCKS, bs, bs), F32),
            pltpu.VMEM((len(CHUNKS), height, bs // 2), F32),
        ],
        compiler_params=pltpu.CompilerParams(vmem_limit_bytes=VMEM_LIMIT),
        name="gram",
    )(unfolding, start)


def inverse_cholesky(inner):
    order = inner.shape[0]
    groups = order // 8
    shape = (8, order)
    lane = lax.broadcasted_iota(jnp.int32, shape, 1)
    sub = lax.broadcasted_iota(jnp.int32, shape, 0)

    def lanes(value, k):
        return jnp.broadcast_to(value[:, k : k + 1], shape)

    def subs(value, i):
        return jnp.broadcast_to(value[i : i + 1, :], shape)

    def reciprocal(value):
        guess = pl.reciprocal(value, approx=True)
        return guess * (2.0 - value * guess)

    rows = [inner[8 * m : 8 * m + 8, :] for m in range(groups)]
    result = []
    for b in range(groups):
        first = 8 * b
        inside = (lane >= first) & (lane < first + 8)
        own = rows[b]
        column = [lanes(own, first + k) for k in range(8)]
        s = [[subs(column[k], i) for k in range(i + 1)] for i in range(8)]
        masked = jnp.where(inside, jnp.where(lane == first + sub, 1.0, 0.0), own)
        y = [subs(masked, i) for i in range(8)]
        inverse = [None] * 8
        f = [[None] * 8 for _ in range(8)]
        for k in range(8):
            inverse[k] = reciprocal(s[k][k])
            for i in range(k + 1, 8):
                f[i][k] = s[i][k] * inverse[k]
            for i in range(k + 1, 8):
                for j in range(k + 1, i + 1):
                    s[i][j] = s[i][j] - f[i][k] * s[j][k]
                y[i] = y[i] - f[i][k] * y[k]
        z = [y[k] * inverse[k] for k in range(8)]
        p = list(z)
        for i in range(6, -1, -1):
            for j in range(7, i, -1):
                p[i] = p[i] - f[j][i] * p[j]
        out = y[0] * lax.rsqrt(s[0][0])
        for i in range(1, 8):
            out = jnp.where(sub == i, y[i] * lax.rsqrt(s[i][i]), out)
        result.append(jnp.where(lane <= first + sub, out, 0.0))
        for m in range(b + 1, groups):
            value = jnp.where(inside, 0.0, rows[m])
            if m == b + 1:
                v = [lanes(rows[m], first + k) for k in range(8)]
                for k in range(8):
                    for i in range(k + 1, 8):
                        v[i] = v[i] - f[i][k] * v[k]
                for k in range(8):
                    value = value - v[k] * z[k]
            else:
                for k in range(7, -1, -1):
                    value = value - lanes(rows[m], first + k) * p[k]
            rows[m] = value
    return jnp.concatenate(result, axis=0)


def mm6(left, right, dims):
    return lax.dot_general(
        left, right, dims, precision=lax.Precision.HIGHEST, preferred_element_type=F32
    )


def iterate_kernel(bs, start_ref, *refs):
    count = 2 * len(CHUNKS)
    halves = refs[:count]
    u_hbm, factor_ref, core_ref, packed, g_high, g_low, both_ref, basis, image, u_vmem, sem = refs[count:]
    rank = basis.shape[0]
    half = bs // 2
    copy = pltpu.make_async_copy(u_hbm, u_vmem, sem)
    copy.start()
    core = lax.rem(lax.axis_index("in"), 2)
    slot = {}
    for number, chunk in enumerate(CHUNKS):
        own, other = halves[2 * number : 2 * number + 2]
        part = own.shape[0]
        packed[number, pl.ds(pl.multiple_of(core * part, part), part), :] = own[...]
        packed[number, pl.ds(pl.multiple_of((1 - core) * part, part), part), :] = other[...]
        base = 0
        for j in chunk:
            for i in range(j + 1):
                place = len(slot)
                slot[i, j] = place
                if i == j:
                    left = packed[number, base : base + half, :]
                    base += half
                    right = packed[number, base : base + bs, :]
                    left = jnp.concatenate([left, right[:half].T], axis=0)
                else:
                    left = packed[number, base : base + bs, :]
                    base += bs
                    right = packed[number, base : base + bs, :]
                base += bs
                for lo, value in ((0, left), (half, right)):
                    high, low = split(value)
                    g_high[place, :, lo : lo + half] = high
                    g_low[place, :, lo : lo + half] = low
    both_ref[...] = start_ref[...]

    def body(_, carry):
        for j in range(BLOCKS):
            total = None
            extra = None
            for i in range(BLOCKS):
                pair, dims = ((i, j), NN) if i <= j else ((j, i), NT)
                cols = slice(i * bs, (i + 1) * bs)
                t = mm(both_ref[:, cols], g_high[slot[pair]], dims)
                e = mm(both_ref[:rank, cols], g_low[slot[pair]], dims)
                total = t if total is None else total + t
                extra = e if extra is None else extra + e
            image[:, j * bs : (j + 1) * bs] = total[:rank] + (total[rank:] + extra)
        inner = mm6(image[...], image[...], NT)
        result = mm6(inverse_cholesky(inner), image[...], NN)
        basis[...] = result
        high, low = split(result)
        both_ref[:rank, :] = high
        both_ref[rank:, :] = low
        return carry

    lax.fori_loop(0, ITERS, body, 0)
    factor_ref[...] = basis[...].T
    copy.wait()
    depth = u_vmem.shape[1]
    step = min(512, depth)
    for lo in range(0, depth, step):
        cols = slice(lo, lo + step)
        u_high, u_low = split(u_vmem[:, cols])
        total = mm(both_ref[...], u_high, NN)
        core_ref[:, cols] = total[:rank] + (total[rank:] + mm(both_ref[:rank, :], u_low, NN))


def iterate(start, halves, unfolding):
    rank = start.shape[0] // 2
    order, depth = unfolding.shape
    bs = order // BLOCKS
    blocks = sum(1 + j for chunk in CHUNKS for j in chunk)
    vmem = pl.BlockSpec(memory_space=pltpu.VMEM)
    hbm = pl.BlockSpec(memory_space=pl.ANY)
    return pl.pallas_call(
        functools.partial(iterate_kernel, bs),
        in_specs=[vmem] * (1 + len(halves)) + [hbm],
        out_specs=[vmem, vmem],
        out_shape=[
            jax.ShapeDtypeStruct((order, rank), F32),
            jax.ShapeDtypeStruct((rank, depth), F32),
        ],
        scratch_shapes=[
            pltpu.VMEM((len(CHUNKS), packed_rows(CHUNKS[0], bs), bs // 2), F32),
            pltpu.VMEM((blocks, bs, bs), BF16),
            pltpu.VMEM((blocks, bs, bs), BF16),
            pltpu.VMEM((2 * rank, order), BF16),
            pltpu.VMEM((rank, order), F32),
            pltpu.VMEM((rank, order), F32),
            pltpu.VMEM((order, depth), F32),
            pltpu.SemaphoreType.DMA,
        ],
        compiler_params=pltpu.CompilerParams(vmem_limit_bytes=36 * 1024 * 1024),
        name="iterate",
    )(start, *halves, unfolding)


class Exchange:
    def __init__(self, groups, inner):
        self.groups, self.inner = groups, inner
        grp = [("grp", k) for k in range(groups.bit_length() - 1)]
        rest = [("in", k) for k in range(1, inner.bit_length() - 1)]
        self.orders = (grp + rest, grp[:2][::-1] + grp[2:] + rest)
        self.index = {"grp": lax.axis_index("grp"), "in": lax.axis_index("in")}
        self.core = self.index["in"] & 1

    def swap(self, value, stage):
        pairs = []
        for g in range(self.groups):
            for i in range(self.inner):
                axis, bit = ("in", 0) if stage is None else self.orders[i & 1][stage]
                to = (g ^ (1 << bit), i) if axis == "grp" else (g, i ^ (1 << bit))
                pairs.append((g * self.inner + i, to[0] * self.inner + to[1]))
        return lax.ppermute(value, ("grp", "in"), pairs)

    def bit(self, stage):
        bits = [(self.index[axis] >> k) & 1 for axis, k in (order[stage] for order in self.orders)]
        return jnp.where(self.core == 0, bits[0], bits[1])

    def all_sum(self, sent, kept):
        last = len(self.orders[0]) - 1
        came = self.swap(sent, None)
        for stage in range(last):
            bit = self.bit(stage)
            parts = [x.reshape(2, x.shape[0] // 2, x.shape[1]) for x in (kept, came)]

            def half(place):
                own, new = (lax.dynamic_index_in_dim(x, place, 0, keepdims=False) for x in parts)
                return own + new

            sent, kept = half(1 - bit), half(bit)
            came = self.swap(sent, stage)
        value = kept + came
        value = value + self.swap(value, last)
        for stage in range(last - 1, -1, -1):
            came = self.swap(value, stage)
            bit = self.bit(stage)
            whole = jnp.zeros((2,) + value.shape, value.dtype)
            whole = lax.dynamic_update_index_in_dim(whole, value, bit, 0)
            whole = lax.dynamic_update_index_in_dim(whole, came, 1 - bit, 0)
            value = whole.reshape(-1, value.shape[1])
        return value, self.swap(value, None)


def per_device(groups, inner, unfolding, start_basis):
    *parts, start = gram(unfolding, start_basis)
    exchange = Exchange(groups, inner)
    halves = []
    for number in range(len(CHUNKS)):
        halves += exchange.all_sum(*parts[2 * number : 2 * number + 2])
    factor, core_block = iterate(start, halves, unfolding)
    return (factor, core_block)


def solution(mesh):
    in_specs = (P(None, ("grp", "in")), P())
    out_specs = (P(), P(None, ("grp", "in")))
    body = functools.partial(per_device, mesh.shape["grp"], mesh.shape["in"])
    return jax.shard_map(body, mesh=mesh, in_specs=in_specs, out_specs=out_specs, check_vma=False)
```

```python
import functools

import jax
import jax.numpy as jnp
from jax import lax
from jax.experimental import pallas as pl
from jax.experimental.pallas import tpu as pltpu
from jax.sharding import PartitionSpec as P

ITERS = 3
BLOCKS = 4
F32 = jnp.float32
BF16 = jnp.bfloat16
NT = (((1,), (1,)), ((), ()))
NN = (((1,), (0,)), ((), ()))

CHUNKS = (
    ((0, 1), (0, 2), (1, 2), (0, 3), (1, 3), (2, 3)),
    ((0, 0), (1, 1), (2, 2), (3, 3)),
)


def split(value):
    high = value.astype(BF16)
    low = (value - high.astype(F32)).astype(BF16)
    return high, low


def mm(left, right, dims):
    return lax.dot_general(left, right, dims, preferred_element_type=F32)


def units(chunk, bs):
    for i, j in chunk:
        yield i, j, 0, (bs // 2 if i == j else bs)
        yield i, j, 1, bs


def packed_rows(chunk, bs):
    return sum(rows for *_, rows in units(chunk, bs))


def gram_kernel(bs, steps, u_ref, start_ref, *refs):
    outs = refs[: 2 * len(CHUNKS)]
    start_out, first_ref, second_ref, acc_ref, cross_ref = refs[2 * len(CHUNKS) : 2 * len(CHUNKS) + 5]
    packed_refs = refs[2 * len(CHUNKS) + 5 :]
    buffers = (first_ref, second_ref)
    step = pl.program_id(0)
    depth = u_ref.shape[1]

    def load(ref, part):
        rows = slice(part * bs, (part + 1) * bs)
        high, low = split(u_ref[rows, :])
        ref[rows, 0 * depth : 1 * depth] = high
        ref[rows, 1 * depth : 2 * depth] = high
        ref[rows, 2 * depth : 3 * depth] = low
        ref[rows, 3 * depth : 4 * depth] = high

    def multiply(ref, j):
        above, end = j * bs, (j + 1) * bs
        if j:
            acc_ref[:above, above:end] += mm(
                ref[:above, depth : 4 * depth], ref[above:end, : 3 * depth], NT
            )
        high = ref[above:end, :depth]
        acc_ref[above:end, above:end] += mm(high, high, NT)
        cross_ref[j] += mm(high, ref[above:end, 2 * depth : 3 * depth], NT)

    @pl.when(step == 0)
    def _():
        acc_ref[...] = jnp.zeros_like(acc_ref)
        cross_ref[...] = jnp.zeros_like(cross_ref)
        high, low = split(start_ref[...].T)
        start_out[: high.shape[0], :] = high
        start_out[high.shape[0] :, :] = low
        for part in range(BLOCKS):
            load(buffers[0], part)

    for parity in range(2):

        @pl.when((step > 0) & (step < steps) & (lax.rem(step, 2) == parity))
        def _():
            for j in range(BLOCKS):
                multiply(buffers[1 - parity], BLOCKS - 1 - j)
                load(buffers[parity], j)

    @pl.when(step == steps)
    def _():
        for j in range(BLOCKS):
            multiply(buffers[(steps - 1) % 2], j)
        core = lax.rem(lax.axis_index("in"), 2)
        for j in range(BLOCKS):
            above, end = j * bs, (j + 1) * bs
            acc_ref[above:end, above:end] += cross_ref[j] + cross_ref[j].T
        for number, (chunk, packed) in enumerate(zip(CHUNKS, packed_refs)):
            base = 0
            for i, j, half, height in units(chunk, bs):
                left = j * bs + half * (bs // 2)
                packed[base : base + height, :] = acc_ref[
                    i * bs : i * bs + height, left : left + bs // 2
                ]
                base += height
            sent, kept = outs[2 * number : 2 * number + 2]
            part = sent.shape[0]
            sent[...] = packed[pl.ds(pl.multiple_of((1 - core) * part, part), part), :]
            kept[...] = packed[pl.ds(pl.multiple_of(core * part, part), part), :]


def gram(unfolding, start):
    order, depth = unfolding.shape
    rank = start.shape[1]
    bs = order // BLOCKS
    width = min(512, depth)
    steps = depth // width
    heights = [packed_rows(chunk, bs) for chunk in CHUNKS]
    halves = [(height // 2, bs // 2) for height in heights for _ in range(2)]
    return pl.pallas_call(
        functools.partial(gram_kernel, bs, steps),
        grid=(steps + 1,),
        in_specs=[
            pl.BlockSpec((order, width), lambda k: (0, jnp.minimum(k, steps - 1))),
            pl.BlockSpec((order, rank), lambda k: (0, 0)),
        ],
        out_specs=[pl.BlockSpec(shape, lambda k: (0, 0)) for shape in halves]
        + [pl.BlockSpec((2 * rank, order), lambda k: (0, 0))],
        out_shape=[jax.ShapeDtypeStruct(shape, F32) for shape in halves]
        + [jax.ShapeDtypeStruct((2 * rank, order), BF16)],
        scratch_shapes=[
            pltpu.VMEM((order, 4 * width), BF16),
            pltpu.VMEM((order, 4 * width), BF16),
            pltpu.VMEM((order, order), F32),
            pltpu.VMEM((BLOCKS, bs, bs), F32),
        ]
        + [pltpu.VMEM((height, bs // 2), F32) for height in heights],
        compiler_params=pltpu.CompilerParams(vmem_limit_bytes=60 * 1024 * 1024),
        name="gram",
    )(unfolding, start)


def inverse_cholesky(inner):
    order = inner.shape[0]
    groups = order // 8
    shape = (8, order)
    lane = lax.broadcasted_iota(jnp.int32, shape, 1)
    sub = lax.broadcasted_iota(jnp.int32, shape, 0)

    def lanes(value, k):
        return jnp.broadcast_to(value[:, k : k + 1], shape)

    def subs(value, i):
        return jnp.broadcast_to(value[i : i + 1, :], shape)

    def reciprocal(value):
        guess = pl.reciprocal(value, approx=True)
        return guess * (2.0 - value * guess)

    rows = [inner[8 * m : 8 * m + 8, :] for m in range(groups)]
    result = []
    for b in range(groups):
        first = 8 * b
        inside = (lane >= first) & (lane < first + 8)
        own = rows[b]
        column = [lanes(own, first + k) for k in range(8)]
        s = [[subs(column[k], i) for k in range(i + 1)] for i in range(8)]
        masked = jnp.where(inside, jnp.where(lane == first + sub, 1.0, 0.0), own)
        y = [subs(masked, i) for i in range(8)]
        inverse = [None] * 8
        f = [[None] * 8 for _ in range(8)]
        for k in range(8):
            inverse[k] = reciprocal(s[k][k])
            for i in range(k + 1, 8):
                f[i][k] = s[i][k] * inverse[k]
            for i in range(k + 1, 8):
                for j in range(k + 1, i + 1):
                    s[i][j] = s[i][j] - f[i][k] * s[j][k]
                y[i] = y[i] - f[i][k] * y[k]
        z = [y[k] * inverse[k] for k in range(8)]
        p = list(z)
        for i in range(6, -1, -1):
            for j in range(7, i, -1):
                p[i] = p[i] - f[j][i] * p[j]
        out = y[0] * lax.rsqrt(s[0][0])
        for i in range(1, 8):
            out = jnp.where(sub == i, y[i] * lax.rsqrt(s[i][i]), out)
        result.append(jnp.where(lane <= first + sub, out, 0.0))
        for m in range(b + 1, groups):
            value = jnp.where(inside, 0.0, rows[m])
            if m == b + 1:
                v = [lanes(rows[m], first + k) for k in range(8)]
                for k in range(8):
                    for i in range(k + 1, 8):
                        v[i] = v[i] - f[i][k] * v[k]
                for k in range(8):
                    value = value - v[k] * z[k]
            else:
                for k in range(7, -1, -1):
                    value = value - lanes(rows[m], first + k) * p[k]
            rows[m] = value
    return jnp.concatenate(result, axis=0)


def mm6(left, right, dims):
    return lax.dot_general(
        left, right, dims, precision=lax.Precision.HIGHEST, preferred_element_type=F32
    )


def iterate_kernel(bs, start_ref, *refs):
    count = 2 * len(CHUNKS)
    halves, refs = refs[:count], refs[count:]
    u_hbm, factor_hbm, core_hbm, *refs = refs
    packed_refs, refs = refs[: len(CHUNKS)], refs[len(CHUNKS) :]
    g_high, g_low, both_ref, basis, image, u_vmem, factor_ref, core_ref, sem, out_sem = refs
    rank = basis.shape[0]
    half = bs // 2
    copy = pltpu.make_async_copy(u_hbm, u_vmem, sem)
    copy.start()
    core = lax.rem(lax.axis_index("in"), 2)
    slot = {}
    for number, (chunk, packed) in enumerate(zip(CHUNKS, packed_refs)):
        own, other = halves[2 * number : 2 * number + 2]
        part = own.shape[0]
        packed[pl.ds(pl.multiple_of(core * part, part), part), :] = own[...]
        packed[pl.ds(pl.multiple_of((1 - core) * part, part), part), :] = other[...]
        base = 0
        for i, j, side, height in units(chunk, bs):
            value = packed[base : base + height, :]
            base += height
            place = slot.setdefault((i, j), len(slot))
            high, low = split(value)
            g_high[place, :height, side * half : (side + 1) * half] = high
            g_low[place, :height, side * half : (side + 1) * half] = low
            if i == j and side:
                high, low = split(value[:half].T)
                g_high[place, half:, :half] = high
                g_low[place, half:, :half] = low
    both_ref[...] = start_ref[...]

    def body(_, carry):
        for j in range(BLOCKS):
            total = None
            extra = None
            for i in range(BLOCKS):
                pair, dims = ((i, j), NN) if i <= j else ((j, i), NT)
                cols = slice(i * bs, (i + 1) * bs)
                t = mm(both_ref[:, cols], g_high[slot[pair]], dims)
                e = mm(both_ref[:rank, cols], g_low[slot[pair]], dims)
                total = t if total is None else total + t
                extra = e if extra is None else extra + e
            image[:, j * bs : (j + 1) * bs] = total[:rank] + (total[rank:] + extra)
        inner = mm6(image[...], image[...], NT)
        result = mm6(inverse_cholesky(inner), image[...], NN)
        basis[...] = result
        high, low = split(result)
        both_ref[:rank, :] = high
        both_ref[rank:, :] = low
        return carry

    lax.fori_loop(0, ITERS, body, 0)
    factor_ref[...] = basis[...].T
    depth = u_vmem.shape[1]
    step = min(512, depth)
    outs = [pltpu.make_async_copy(factor_ref, factor_hbm, out_sem.at[0])]
    outs[0].start()
    copy.wait()
    for number, lo in enumerate(range(0, depth, step)):
        cols = slice(lo, lo + step)
        u_high, u_low = split(u_vmem[:, cols])
        total = mm(both_ref[...], u_high, NN)
        core_ref[:, cols] = total[:rank] + (total[rank:] + mm(both_ref[:rank, :], u_low, NN))
        outs.append(
            pltpu.make_async_copy(core_ref.at[:, cols], core_hbm.at[:, cols], out_sem.at[number + 1])
        )
        outs[-1].start()
    for out in outs:
        out.wait()


def iterate(start, halves, unfolding):
    rank = start.shape[0] // 2
    order, depth = unfolding.shape
    bs = order // BLOCKS
    blocks = sum(len(chunk) for chunk in CHUNKS)
    vmem = pl.BlockSpec(memory_space=pltpu.VMEM)
    hbm = pl.BlockSpec(memory_space=pl.ANY)
    return pl.pallas_call(
        functools.partial(iterate_kernel, bs),
        in_specs=[vmem] * (1 + len(halves)) + [hbm],
        out_specs=[hbm, hbm],
        out_shape=[
            jax.ShapeDtypeStruct((order, rank), F32),
            jax.ShapeDtypeStruct((rank, depth), F32),
        ],
        scratch_shapes=[pltpu.VMEM((packed_rows(chunk, bs), bs // 2), F32) for chunk in CHUNKS]
        + [
            pltpu.VMEM((blocks, bs, bs), BF16),
            pltpu.VMEM((blocks, bs, bs), BF16),
            pltpu.VMEM((2 * rank, order), BF16),
            pltpu.VMEM((rank, order), F32),
            pltpu.VMEM((rank, order), F32),
            pltpu.VMEM((order, depth), F32),
            pltpu.VMEM((order, rank), F32),
            pltpu.VMEM((rank, depth), F32),
            pltpu.SemaphoreType.DMA,
            pltpu.SemaphoreType.DMA((1 + depth // min(512, depth),)),
        ],
        compiler_params=pltpu.CompilerParams(vmem_limit_bytes=36 * 1024 * 1024),
        name="iterate",
    )(start, *halves, unfolding)


class Exchange:
    def __init__(self, groups, inner, inner_first):
        self.groups, self.inner = groups, inner
        grp = [("grp", k) for k in range(groups.bit_length() - 1)]
        rest = [("in", k) for k in range(1, inner.bit_length() - 1)]
        flipped = grp[:2][::-1] + grp[2:]
        if inner_first:
            self.orders = tuple(rest[:1] + g + rest[1:] for g in (grp, flipped))
        else:
            self.orders = (grp + rest, flipped + rest)
        self.index = {"grp": lax.axis_index("grp"), "in": lax.axis_index("in")}
        self.core = self.index["in"] & 1

    def swap(self, value, stage):
        pairs = []
        for g in range(self.groups):
            for i in range(self.inner):
                axis, bit = ("in", 0) if stage is None else self.orders[i & 1][stage]
                to = (g ^ (1 << bit), i) if axis == "grp" else (g, i ^ (1 << bit))
                pairs.append((g * self.inner + i, to[0] * self.inner + to[1]))
        return lax.ppermute(value, ("grp", "in"), pairs)

    def bit(self, stage):
        bits = [(self.index[axis] >> k) & 1 for axis, k in (order[stage] for order in self.orders)]
        return jnp.where(self.core == 0, bits[0], bits[1])

    def all_sum(self, sent, kept):
        last = len(self.orders[0]) - 1
        came = self.swap(sent, None)
        for stage in range(last):
            bit = self.bit(stage)
            parts = [x.reshape(2, x.shape[0] // 2, x.shape[1]) for x in (kept, came)]

            def half(place):
                own, new = (lax.dynamic_index_in_dim(x, place, 0, keepdims=False) for x in parts)
                return own + new

            sent, kept = half(1 - bit), half(bit)
            came = self.swap(sent, stage)
        value = kept + came
        value = value + self.swap(value, last)
        for stage in range(last - 1, -1, -1):
            came = self.swap(value, stage)
            bit = self.bit(stage)
            whole = jnp.zeros((2,) + value.shape, value.dtype)
            whole = lax.dynamic_update_index_in_dim(whole, value, bit, 0)
            whole = lax.dynamic_update_index_in_dim(whole, came, 1 - bit, 0)
            value = whole.reshape(-1, value.shape[1])
        return value, self.swap(value, None)


def per_device(groups, inner, unfolding, start_basis):
    *parts, start = gram(unfolding, start_basis)
    halves = []
    for number in range(len(CHUNKS)):
        exchange = Exchange(groups, inner, number > 0)
        halves += exchange.all_sum(*parts[2 * number : 2 * number + 2])
    factor, core_block = iterate(start, halves, unfolding)
    return (factor, core_block)


def solution(mesh):
    in_specs = (P(None, ("grp", "in")), P())
    out_specs = (P(), P(None, ("grp", "in")))
    body = functools.partial(per_device, mesh.shape["grp"], mesh.shape["in"])
    return jax.shard_map(body, mesh=mesh, in_specs=in_specs, out_specs=out_specs, check_vma=False)
```

```python
import functools

import jax
import jax.numpy as jnp
from jax import lax
from jax.experimental import pallas as pl
from jax.experimental.pallas import tpu as pltpu
from jax.sharding import PartitionSpec as P

ITERS = 3
BLOCKS = 4
F32 = jnp.float32
BF16 = jnp.bfloat16
NT = (((1,), (1,)), ((), ()))
NN = (((1,), (0,)), ((), ()))

CHUNKS = (
    ((0, 3), (1, 3), (2, 3), (3, 3), (0, 0)),
    ((0, 2), (1, 2), (2, 2), (0, 1), (1, 1)),
)


def split(value):
    high = value.astype(BF16)
    low = (value - high.astype(F32)).astype(BF16)
    return high, low


def mm(left, right, dims):
    return lax.dot_general(left, right, dims, preferred_element_type=F32)


def units(chunk, bs):
    for i, j in chunk:
        yield i, j, 0, (bs // 2 if i == j else bs)
        yield i, j, 1, bs


def packed_rows(chunk, bs):
    return sum(rows for *_, rows in units(chunk, bs))


def gram_kernel(bs, widths, u_hbm, *refs):
    count = len(CHUNKS)
    outs, packed_refs = refs[: 2 * count], refs[2 * count : 3 * count]
    u_ref, parts_ref, acc_ref, cross_ref, sems = refs[3 * count :]
    copies = []
    first = 0
    for number, width in enumerate(widths):
        cols = slice(first, first + width)
        copies.append(pltpu.make_async_copy(u_hbm.at[:, cols], u_ref.at[:, cols], sems.at[number]))
        copies[-1].start()
        first += width

    def add(ref, place, value, new):
        ref[place] = value if new else ref[place] + value

    first = 0
    for number, width in enumerate(widths):
        copies[number].wait()
        for j in range(BLOCKS):
            rows = slice(j * bs, (j + 1) * bs)
            high, low = split(u_ref[rows, first : first + width])
            for place, value in enumerate((high, high, low, high)):
                parts_ref[rows, place * width : (place + 1) * width] = value
        first += width
        for j in range(BLOCKS):
            above, end = j * bs, (j + 1) * bs
            if j:
                value = mm(
                    parts_ref[:above, width : 4 * width], parts_ref[above:end, : 3 * width], NT
                )
                add(acc_ref, (slice(0, above), slice(above, end)), value, number == 0)
            high = parts_ref[above:end, :width]
            low = parts_ref[above:end, 2 * width : 3 * width]
            own = (slice(above, end), slice(above, end))
            add(acc_ref, own, mm(high, high, NT), number == 0)
            add(cross_ref, j, mm(high, low, NT), number == 0)

    core = lax.rem(lax.axis_index("in"), 2)
    for j in range(BLOCKS):
        above, end = j * bs, (j + 1) * bs
        acc_ref[above:end, above:end] += cross_ref[j] + cross_ref[j].T
    for number, (chunk, packed) in enumerate(zip(CHUNKS, packed_refs)):
        base = 0
        for i, j, half, height in units(chunk, bs):
            left = j * bs + half * (bs // 2)
            packed[base : base + height, :] = acc_ref[
                i * bs : i * bs + height, left : left + bs // 2
            ]
            base += height
        sent, kept = outs[2 * number : 2 * number + 2]
        part = sent.shape[0]
        sent[...] = packed[pl.ds(pl.multiple_of((1 - core) * part, part), part), :]
        kept[...] = packed[pl.ds(pl.multiple_of(core * part, part), part), :]


def gram(unfolding):
    order, depth = unfolding.shape
    bs = order // BLOCKS
    widths = (depth // 8, 3 * depth // 8, depth // 2)
    heights = [packed_rows(chunk, bs) for chunk in CHUNKS]
    halves = [(height // 2, bs // 2) for height in heights for _ in range(2)]
    return pl.pallas_call(
        functools.partial(gram_kernel, bs, widths),
        in_specs=[pl.BlockSpec(memory_space=pl.ANY)],
        out_specs=[pl.BlockSpec(memory_space=pltpu.VMEM)] * len(halves),
        out_shape=[pltpu.VMEM(shape, F32) for shape in halves],
        scratch_shapes=[pltpu.VMEM((height, bs // 2), F32) for height in heights]
        + [
            pltpu.VMEM((order, depth), F32),
            pltpu.VMEM((order, 4 * max(widths)), BF16),
            pltpu.VMEM((order, order), F32),
            pltpu.VMEM((BLOCKS, bs, bs), F32),
            pltpu.SemaphoreType.DMA((len(widths),)),
        ],
        compiler_params=pltpu.CompilerParams(vmem_limit_bytes=50 * 1024 * 1024),
        name="gram",
    )(unfolding)


def inverse_cholesky(inner):
    order = inner.shape[0]
    size = min(16, order)
    shape = (8, order)
    lane = lax.broadcasted_iota(jnp.int32, shape, 1)
    sub = lax.broadcasted_iota(jnp.int32, shape, 0)

    def lanes(value, k):
        return jnp.broadcast_to(value[:, k : k + 1], shape)

    def subs(value, i):
        return jnp.broadcast_to(value[i : i + 1, :], shape)

    def reciprocal(value):
        guess = pl.reciprocal(value, approx=True)
        return guess * (2.0 - value * guess)

    rows = [inner[m : m + 8, :] for m in range(0, order, 8)]
    result = []
    for first in range(0, order, size):
        inside = (lane >= first) & (lane < first + size)
        own = rows[first // 8 : (first + size) // 8]
        s = [[None] * (i + 1) for i in range(size)]
        for k in range(size):
            for g in range(k // 8, size // 8):
                column = lanes(own[g], first + k)
                for i in range(max(k, 8 * g), 8 * g + 8):
                    s[i][k] = subs(column, i - 8 * g)
        y = []
        for g in range(size // 8):
            unit = jnp.where(lane == first + 8 * g + sub, 1.0, 0.0)
            masked = jnp.where(inside, unit, own[g])
            y += [subs(masked, i) for i in range(8)]
        inverse = [None] * size
        f = [[None] * size for _ in range(size)]
        for k in range(size):
            inverse[k] = reciprocal(s[k][k])
            for i in range(k + 1, size):
                f[i][k] = s[i][k] * inverse[k]
            for i in range(k + 1, size):
                for j in range(k + 1, i + 1):
                    s[i][j] = s[i][j] - f[i][k] * s[j][k]
                y[i] = y[i] - f[i][k] * y[k]
        p = [y[k] * inverse[k] for k in range(size)]
        for j in range(size - 1, 0, -1):
            for i in range(j - 1, -1, -1):
                p[i] = p[i] - f[j][i] * p[j]
        for g in range(size // 8):
            out = y[8 * g] * lax.rsqrt(s[8 * g][8 * g])
            for i in range(1, 8):
                out = jnp.where(sub == i, y[8 * g + i] * lax.rsqrt(s[8 * g + i][8 * g + i]), out)
            result.append(jnp.where(lane <= first + 8 * g + sub, out, 0.0))
        for m in range((first + size) // 8, order // 8):
            value = jnp.where(inside, 0.0, rows[m])
            for k in range(size - 1, -1, -1):
                value = value - lanes(rows[m], first + k) * p[k]
            rows[m] = value
    return jnp.concatenate(result, axis=0)


def mm6(left, right, dims):
    return lax.dot_general(
        left, right, dims, precision=lax.Precision.HIGHEST, preferred_element_type=F32
    )


def iterate_kernel(bs, start_hbm, *refs):
    count = 2 * len(CHUNKS)
    halves, refs = refs[:count], refs[count:]
    u_hbm, factor_hbm, core_hbm, *refs = refs
    packed_refs, refs = refs[: len(CHUNKS)], refs[len(CHUNKS) :]
    g_high, g_low, both_ref, basis, image, u_vmem, factor_ref, core_ref, sems, out_sem = refs
    rank = basis.shape[0]
    half = bs // 2
    start_copy = pltpu.make_async_copy(start_hbm, factor_ref, sems.at[0])
    start_copy.start()
    copy = pltpu.make_async_copy(u_hbm, u_vmem, sems.at[1])
    copy.start()
    core = lax.rem(lax.axis_index("in"), 2)
    slot = {}
    for number, (chunk, packed) in enumerate(zip(CHUNKS, packed_refs)):
        own, other = halves[2 * number : 2 * number + 2]
        part = own.shape[0]
        packed[pl.ds(pl.multiple_of(core * part, part), part), :] = own[...]
        packed[pl.ds(pl.multiple_of((1 - core) * part, part), part), :] = other[...]
        base = 0
        for i, j, side, height in units(chunk, bs):
            value = packed[base : base + height, :]
            base += height
            place = slot.setdefault((i, j), len(slot))
            high, low = split(value)
            g_high[place, :height, side * half : (side + 1) * half] = high
            g_low[place, :height, side * half : (side + 1) * half] = low
            if i == j and side:
                high, low = split(value[:half].T)
                g_high[place, half:, :half] = high
                g_low[place, half:, :half] = low
    start_copy.wait()
    high, low = split(factor_ref[...].T)
    both_ref[:rank, :] = high
    both_ref[rank:, :] = low

    def body(_, carry):
        for j in range(BLOCKS):
            total = None
            extra = None
            for i in range(BLOCKS):
                pair, dims = ((i, j), NN) if i <= j else ((j, i), NT)
                cols = slice(i * bs, (i + 1) * bs)
                t = mm(both_ref[:, cols], g_high[slot[pair]], dims)
                e = mm(both_ref[:rank, cols], g_low[slot[pair]], dims)
                total = t if total is None else total + t
                extra = e if extra is None else extra + e
            image[:, j * bs : (j + 1) * bs] = total[:rank] + (total[rank:] + extra)
        inner = mm6(image[...], image[...], NT)
        result = mm6(inverse_cholesky(inner), image[...], NN)
        basis[...] = result
        high, low = split(result)
        both_ref[:rank, :] = high
        both_ref[rank:, :] = low
        return carry

    lax.fori_loop(0, ITERS, body, 0)
    factor_ref[...] = basis[...].T
    depth = u_vmem.shape[1]
    step = min(512, depth)
    outs = [pltpu.make_async_copy(factor_ref, factor_hbm, out_sem.at[0])]
    outs[0].start()
    copy.wait()
    for number, lo in enumerate(range(0, depth, step)):
        cols = slice(lo, lo + step)
        u_high, u_low = split(u_vmem[:, cols])
        total = mm(both_ref[...], u_high, NN)
        core_ref[:, cols] = total[:rank] + (total[rank:] + mm(both_ref[:rank, :], u_low, NN))
        outs.append(
            pltpu.make_async_copy(core_ref.at[:, cols], core_hbm.at[:, cols], out_sem.at[number + 1])
        )
        outs[-1].start()
    for out in outs:
        out.wait()


def iterate(start, halves, unfolding):
    order, rank = start.shape
    depth = unfolding.shape[1]
    bs = order // BLOCKS
    blocks = sum(len(chunk) for chunk in CHUNKS)
    vmem = pl.BlockSpec(memory_space=pltpu.VMEM)
    hbm = pl.BlockSpec(memory_space=pl.ANY)
    return pl.pallas_call(
        functools.partial(iterate_kernel, bs),
        in_specs=[hbm] + [vmem] * len(halves) + [hbm],
        out_specs=[hbm, hbm],
        out_shape=[
            jax.ShapeDtypeStruct((order, rank), F32),
            jax.ShapeDtypeStruct((rank, depth), F32),
        ],
        scratch_shapes=[pltpu.VMEM((packed_rows(chunk, bs), bs // 2), F32) for chunk in CHUNKS]
        + [
            pltpu.VMEM((blocks, bs, bs), BF16),
            pltpu.VMEM((blocks, bs, bs), BF16),
            pltpu.VMEM((2 * rank, order), BF16),
            pltpu.VMEM((rank, order), F32),
            pltpu.VMEM((rank, order), F32),
            pltpu.VMEM((order, depth), F32),
            pltpu.VMEM((order, rank), F32),
            pltpu.VMEM((rank, depth), F32),
            pltpu.SemaphoreType.DMA((2,)),
            pltpu.SemaphoreType.DMA((1 + depth // min(512, depth),)),
        ],
        compiler_params=pltpu.CompilerParams(vmem_limit_bytes=36 * 1024 * 1024),
        name="iterate",
    )(start, *halves, unfolding)


class Exchange:
    def __init__(self, groups, inner):
        self.groups, self.inner = groups, inner
        grp = [("grp", k) for k in range(groups.bit_length() - 1)]
        rest = [("in", k) for k in range(1, inner.bit_length() - 1)]
        self.orders = (grp + rest, grp[:2][::-1] + grp[2:] + rest)
        self.index = {"grp": lax.axis_index("grp"), "in": lax.axis_index("in")}
        self.core = self.index["in"] & 1

    def swap(self, value, stage):
        pairs = []
        for g in range(self.groups):
            for i in range(self.inner):
                axis, bit = ("in", 0) if stage is None else self.orders[i & 1][stage]
                to = (g ^ (1 << bit), i) if axis == "grp" else (g, i ^ (1 << bit))
                pairs.append((g * self.inner + i, to[0] * self.inner + to[1]))
        return lax.ppermute(value, ("grp", "in"), pairs)

    def bit(self, stage):
        bits = [(self.index[axis] >> k) & 1 for axis, k in (order[stage] for order in self.orders)]
        return jnp.where(self.core == 0, bits[0], bits[1])

    def all_sum(self, sent, kept):
        last = len(self.orders[0]) - 1
        came = self.swap(sent, None)
        for stage in range(last):
            bit = self.bit(stage)
            parts = [x.reshape(2, x.shape[0] // 2, x.shape[1]) for x in (kept, came)]

            def half(place):
                own, new = (lax.dynamic_index_in_dim(x, place, 0, keepdims=False) for x in parts)
                return own + new

            sent, kept = half(1 - bit), half(bit)
            came = self.swap(sent, stage)
        value = kept + came
        value = value + self.swap(value, last)
        for stage in range(last - 1, -1, -1):
            came = self.swap(value, stage)
            bit = self.bit(stage)
            whole = jnp.zeros((2,) + value.shape, value.dtype)
            whole = lax.dynamic_update_index_in_dim(whole, value, bit, 0)
            whole = lax.dynamic_update_index_in_dim(whole, came, 1 - bit, 0)
            value = whole.reshape(-1, value.shape[1])
        return value, self.swap(value, None)


def per_device(groups, inner, unfolding, start_basis):
    parts = gram(unfolding)
    exchange = Exchange(groups, inner)
    halves = []
    for number in range(len(CHUNKS)):
        halves += exchange.all_sum(*parts[2 * number : 2 * number + 2])
    factor, core_block = iterate(start_basis, halves, unfolding)
    return (factor, core_block)


def solution(mesh):
    in_specs = (P(None, ("grp", "in")), P())
    out_specs = (P(), P(None, ("grp", "in")))
    body = functools.partial(per_device, mesh.shape["grp"], mesh.shape["in"])
    return jax.shard_map(body, mesh=mesh, in_specs=in_specs, out_specs=out_specs, check_vma=False)
```

```python
import functools

import jax
import jax.numpy as jnp
from jax import lax
from jax.experimental import pallas as pl
from jax.experimental.pallas import tpu as pltpu
from jax.sharding import PartitionSpec as P

ITERS = 3
BLOCKS = 4
F32 = jnp.float32
BF16 = jnp.bfloat16
NT = (((1,), (1,)), ((), ()))
NN = (((1,), (0,)), ((), ()))

CHUNKS = (
    ((0, 3), (1, 3), (2, 3), (3, 3), (0, 0)),
    ((0, 2), (1, 2), (2, 2), (0, 1), (1, 1)),
)


def split(value):
    high = value.astype(BF16)
    low = (value - high.astype(F32)).astype(BF16)
    return high, low


def split3(value):
    high = value.astype(BF16)
    return high, split(value - high.astype(F32))


def mm(left, right, dims):
    return lax.dot_general(left, right, dims, preferred_element_type=F32)


def units(chunk, bs):
    for i, j in chunk:
        yield i, j, 0, (bs // 2 if i == j else bs)
        yield i, j, 1, bs


def packed_rows(chunk, bs):
    return sum(rows for *_, rows in units(chunk, bs))


def gram_kernel(bs, widths, u_hbm, *refs):
    count = len(CHUNKS)
    outs, packed_refs = refs[: 2 * count], refs[2 * count : 3 * count]
    u_ref, parts_ref, acc_ref, cross_ref, sems = refs[3 * count :]
    copies = []
    first = 0
    for number, width in enumerate(widths):
        cols = slice(first, first + width)
        copies.append(pltpu.make_async_copy(u_hbm.at[:, cols], u_ref.at[:, cols], sems.at[number]))
        copies[-1].start()
        first += width

    order = BLOCKS * bs

    def high(i, end):
        return slice(order + i * bs, order + end * bs)

    def low(i):
        return slice(order - (i + 1) * bs, order - i * bs)

    first = 0
    for number, width in enumerate(widths):
        copies[number].wait()
        for j in range(BLOCKS):
            upper, lower = split(u_ref[j * bs : (j + 1) * bs, first : first + width])
            parts_ref[high(j, j + 1), :width] = upper
            parts_ref[low(j), :width] = lower
        first += width
        for j in range(BLOCKS):
            above, end = j * bs, (j + 1) * bs
            own = (slice(above, end), slice(above, end))
            value = mm(parts_ref[order - end : order + end, :width], parts_ref[high(j, j + 1), :width], NT)
            diagonal, cross = value[2 * end - bs :], value[:bs]
            if number == 0:
                acc_ref[own] = diagonal
                cross_ref[j] = cross
            else:
                acc_ref[own] += diagonal
                cross_ref[j] += cross
            if j:
                more = mm(parts_ref[high(0, j), :width], parts_ref[low(j), :width], NT)
                for i in range(j):
                    place = (slice(i * bs, (i + 1) * bs), slice(above, end))
                    both = value[end + i * bs : end + (i + 1) * bs] + value[end - (i + 1) * bs : end - i * bs]
                    both += more[i * bs : (i + 1) * bs]
                    acc_ref[place] = both if number == 0 else acc_ref[place] + both

    core = lax.rem(lax.axis_index("in"), 2)
    for j in range(BLOCKS):
        above, end = j * bs, (j + 1) * bs
        acc_ref[above:end, above:end] += cross_ref[j] + cross_ref[j].T
    for number, (chunk, packed) in enumerate(zip(CHUNKS, packed_refs)):
        base = 0
        for i, j, half, height in units(chunk, bs):
            left = j * bs + half * (bs // 2)
            packed[base : base + height, :] = acc_ref[
                i * bs : i * bs + height, left : left + bs // 2
            ]
            base += height
        sent, kept = outs[2 * number : 2 * number + 2]
        part = sent.shape[0]
        sent[...] = packed[pl.ds(pl.multiple_of((1 - core) * part, part), part), :]
        kept[...] = packed[pl.ds(pl.multiple_of(core * part, part), part), :]


def gram(unfolding):
    order, depth = unfolding.shape
    bs = order // BLOCKS
    widths = (depth // 8, 3 * depth // 8, depth // 2)
    heights = [packed_rows(chunk, bs) for chunk in CHUNKS]
    halves = [(height // 2, bs // 2) for height in heights for _ in range(2)]
    return pl.pallas_call(
        functools.partial(gram_kernel, bs, widths),
        in_specs=[pl.BlockSpec(memory_space=pl.ANY)],
        out_specs=[pl.BlockSpec(memory_space=pltpu.VMEM)] * len(halves),
        out_shape=[pltpu.VMEM(shape, F32) for shape in halves],
        scratch_shapes=[pltpu.VMEM((height, bs // 2), F32) for height in heights]
        + [
            pltpu.VMEM((order, depth), F32),
            pltpu.VMEM((2 * order, max(widths)), BF16),
            pltpu.VMEM((order, order), F32),
            pltpu.VMEM((BLOCKS, bs, bs), F32),
            pltpu.SemaphoreType.DMA((len(widths),)),
        ],
        compiler_params=pltpu.CompilerParams(vmem_limit_bytes=50 * 1024 * 1024),
        name="gram",
    )(unfolding)


def inverse_cholesky(inner):
    order = inner.shape[0]
    size = min(16, order)
    shape = (8, order)
    lane = lax.broadcasted_iota(jnp.int32, shape, 1)
    sub = lax.broadcasted_iota(jnp.int32, shape, 0)

    def lanes(value, k):
        return jnp.broadcast_to(value[:, k : k + 1], shape)

    def subs(value, i):
        return jnp.broadcast_to(value[i : i + 1, :], shape)

    def reciprocal(value):
        guess = pl.reciprocal(value, approx=True)
        return guess * (2.0 - value * guess)

    rows = [inner[m : m + 8, :] for m in range(0, order, 8)]
    result = []
    for first in range(0, order, size):
        inside = (lane >= first) & (lane < first + size)
        own = rows[first // 8 : (first + size) // 8]
        s = [[None] * (i + 1) for i in range(size)]
        for k in range(size):
            for g in range(k // 8, size // 8):
                column = lanes(own[g], first + k)
                for i in range(max(k, 8 * g), 8 * g + 8):
                    s[i][k] = subs(column, i - 8 * g)
        y = []
        for g in range(size // 8):
            unit = jnp.where(lane == first + 8 * g + sub, 1.0, 0.0)
            masked = jnp.where(inside, unit, own[g])
            y += [subs(masked, i) for i in range(8)]
        inverse = [None] * size
        f = [[None] * size for _ in range(size)]
        for k in range(size):
            inverse[k] = reciprocal(s[k][k])
            for i in range(k + 1, size):
                f[i][k] = s[i][k] * inverse[k]
            for i in range(k + 1, size):
                for j in range(k + 1, i + 1):
                    s[i][j] = s[i][j] - f[i][k] * s[j][k]
                y[i] = y[i] - f[i][k] * y[k]
        p = [y[k] * inverse[k] for k in range(size)]
        for j in range(size - 1, 0, -1):
            for i in range(j - 1, -1, -1):
                p[i] = p[i] - f[j][i] * p[j]
        for g in range(size // 8):
            out = y[8 * g] * lax.rsqrt(s[8 * g][8 * g])
            for i in range(1, 8):
                out = jnp.where(sub == i, y[8 * g + i] * lax.rsqrt(s[8 * g + i][8 * g + i]), out)
            result.append(jnp.where(lane <= first + 8 * g + sub, out, 0.0))
        for m in range((first + size) // 8, order // 8):
            value = jnp.where(inside, 0.0, rows[m])
            for k in range(size - 1, -1, -1):
                value = value - lanes(rows[m], first + k) * p[k]
            rows[m] = value
    return jnp.concatenate(result, axis=0)


def iterate_kernel(bs, start_hbm, *refs):
    count = 2 * len(CHUNKS)
    halves, refs = refs[:count], refs[count:]
    u_hbm, factor_hbm, core_hbm, *refs = refs
    packed_refs, refs = refs[: len(CHUNKS)], refs[len(CHUNKS) :]
    g_high, g_low, both_ref, basis, parts_ref, u_vmem, factor_ref, core_ref, sems, out_sem = refs
    rank = basis.shape[0]
    half = bs // 2
    start_copy = pltpu.make_async_copy(start_hbm, factor_ref, sems.at[0])
    start_copy.start()
    copy = pltpu.make_async_copy(u_hbm, u_vmem, sems.at[1])
    copy.start()
    core = lax.rem(lax.axis_index("in"), 2)
    for number, (chunk, packed) in enumerate(zip(CHUNKS, packed_refs)):
        own, other = halves[2 * number : 2 * number + 2]
        part = own.shape[0]
        packed[pl.ds(pl.multiple_of(core * part, part), part), :] = own[...]
        packed[pl.ds(pl.multiple_of((1 - core) * part, part), part), :] = other[...]
        base = 0
        for i, j, side, height in units(chunk, bs):
            value = packed[base : base + height, :]
            base += height
            place = (slice(i * bs, i * bs + height), slice(j * bs + side * half, j * bs + (side + 1) * half))
            g_high[place], g_low[place] = split(value)
            if i == j and side:
                place = (slice(i * bs + half, (i + 1) * bs), slice(j * bs, j * bs + half))
                g_high[place], g_low[place] = split(value[:half].T)
    start_copy.wait()
    high, low = split(factor_ref[...].T)
    both_ref[:rank, :] = high
    both_ref[rank:, :] = low

    def body(_, carry):
        for j in range(BLOCKS):
            above, end = j * bs, (j + 1) * bs
            total = mm(both_ref[:, :end], g_high[:end, above:end], NN)
            extra = mm(both_ref[:rank, :end], g_low[:end, above:end], NN)
            if j < BLOCKS - 1:
                total += mm(both_ref[:, end:], g_high[above:end, end:], NT)
                extra += mm(both_ref[:rank, end:], g_low[above:end, end:], NT)
            value = total[:rank] + (total[rank:] + extra)
            high, rest = split3(value)
            parts_ref[:rank, above:end] = rest[0]
            parts_ref[rank : 2 * rank, above:end] = high
            parts_ref[2 * rank :, above:end] = rest[1]
        product = mm(parts_ref[...], parts_ref[: 2 * rank, :], NT)
        cross = product[2 * rank :, rank:]
        inner = product[rank : 2 * rank, rank:] + (
            (product[:rank, rank:] + product[rank : 2 * rank, :rank])
            + (product[:rank, :rank] + (cross + cross.T))
        )
        high, (middle, low) = split3(inverse_cholesky(inner))
        left = jnp.concatenate(
            [
                jnp.concatenate([middle, high], axis=1),
                jnp.concatenate([high, middle], axis=1),
            ],
            axis=0,
        )
        last = jnp.concatenate([low, high], axis=1)
        for j in range(BLOCKS):
            cols = slice(j * bs, (j + 1) * bs)
            product = mm(left, parts_ref[: 2 * rank, cols], NN)
            product = product[:rank] + (product[rank:] + mm(last, parts_ref[rank:, cols], NN))
            basis[:, cols] = product
            both_ref[:rank, cols], both_ref[rank:, cols] = split(product)
        return carry

    lax.fori_loop(0, ITERS, body, 0)
    factor_ref[...] = basis[...].T
    depth = u_vmem.shape[1]
    step = min(512, depth)
    outs = [pltpu.make_async_copy(factor_ref, factor_hbm, out_sem.at[0])]
    outs[0].start()
    copy.wait()
    for number, lo in enumerate(range(0, depth, step)):
        cols = slice(lo, lo + step)
        u_high, u_low = split(u_vmem[:, cols])
        total = mm(both_ref[...], u_high, NN)
        core_ref[:, cols] = total[:rank] + (total[rank:] + mm(both_ref[:rank, :], u_low, NN))
        outs.append(
            pltpu.make_async_copy(core_ref.at[:, cols], core_hbm.at[:, cols], out_sem.at[number + 1])
        )
        outs[-1].start()
    for out in outs:
        out.wait()


def iterate(start, halves, unfolding):
    order, rank = start.shape
    depth = unfolding.shape[1]
    bs = order // BLOCKS
    vmem = pl.BlockSpec(memory_space=pltpu.VMEM)
    hbm = pl.BlockSpec(memory_space=pl.ANY)
    return pl.pallas_call(
        functools.partial(iterate_kernel, bs),
        in_specs=[hbm] + [vmem] * len(halves) + [hbm],
        out_specs=[hbm, hbm],
        out_shape=[
            jax.ShapeDtypeStruct((order, rank), F32),
            jax.ShapeDtypeStruct((rank, depth), F32),
        ],
        scratch_shapes=[pltpu.VMEM((packed_rows(chunk, bs), bs // 2), F32) for chunk in CHUNKS]
        + [
            pltpu.VMEM((order, order), BF16),
            pltpu.VMEM((order, order), BF16),
            pltpu.VMEM((2 * rank, order), BF16),
            pltpu.VMEM((rank, order), F32),
            pltpu.VMEM((3 * rank, order), BF16),
            pltpu.VMEM((order, depth), F32),
            pltpu.VMEM((order, rank), F32),
            pltpu.VMEM((rank, depth), F32),
            pltpu.SemaphoreType.DMA((2,)),
            pltpu.SemaphoreType.DMA((1 + depth // min(512, depth),)),
        ],
        compiler_params=pltpu.CompilerParams(vmem_limit_bytes=36 * 1024 * 1024),
        name="iterate",
    )(start, *halves, unfolding)


class Exchange:
    def __init__(self, groups, inner):
        self.groups, self.inner = groups, inner
        grp = [("grp", k) for k in range(groups.bit_length() - 1)]
        rest = [("in", k) for k in range(1, inner.bit_length() - 1)]
        self.orders = (grp + rest, grp[:2][::-1] + grp[2:] + rest)
        self.index = {"grp": lax.axis_index("grp"), "in": lax.axis_index("in")}
        self.core = self.index["in"] & 1

    def swap(self, value, stage):
        pairs = []
        for g in range(self.groups):
            for i in range(self.inner):
                axis, bit = ("in", 0) if stage is None else self.orders[i & 1][stage]
                to = (g ^ (1 << bit), i) if axis == "grp" else (g, i ^ (1 << bit))
                pairs.append((g * self.inner + i, to[0] * self.inner + to[1]))
        return lax.ppermute(value, ("grp", "in"), pairs)

    def bit(self, stage):
        bits = [(self.index[axis] >> k) & 1 for axis, k in (order[stage] for order in self.orders)]
        return jnp.where(self.core == 0, bits[0], bits[1])

    def all_sum(self, sent, kept):
        last = len(self.orders[0]) - 1
        came = self.swap(sent, None)
        for stage in range(last):
            bit = self.bit(stage)
            parts = [x.reshape(2, x.shape[0] // 2, x.shape[1]) for x in (kept, came)]

            def half(place):
                own, new = (lax.dynamic_index_in_dim(x, place, 0, keepdims=False) for x in parts)
                return own + new

            sent, kept = half(1 - bit), half(bit)
            came = self.swap(sent, stage)
        value = kept + came
        value = value + self.swap(value, last)
        for stage in range(last - 1, -1, -1):
            came = self.swap(value, stage)
            bit = self.bit(stage)
            whole = jnp.zeros((2,) + value.shape, value.dtype)
            whole = lax.dynamic_update_index_in_dim(whole, value, bit, 0)
            whole = lax.dynamic_update_index_in_dim(whole, came, 1 - bit, 0)
            value = whole.reshape(-1, value.shape[1])
        return value, self.swap(value, None)


def per_device(groups, inner, unfolding, start_basis):
    parts = gram(unfolding)
    exchange = Exchange(groups, inner)
    halves = []
    for number in range(len(CHUNKS)):
        halves += exchange.all_sum(*parts[2 * number : 2 * number + 2])
    factor, core_block = iterate(start_basis, halves, unfolding)
    return (factor, core_block)


def solution(mesh):
    in_specs = (P(None, ("grp", "in")), P())
    out_specs = (P(), P(None, ("grp", "in")))
    body = functools.partial(per_device, mesh.shape["grp"], mesh.shape["in"])
    return jax.shard_map(body, mesh=mesh, in_specs=in_specs, out_specs=out_specs, check_vma=False)
```

```python
import functools

import jax
import jax.numpy as jnp
from jax import lax
from jax.experimental import pallas as pl
from jax.experimental.pallas import tpu as pltpu
from jax.sharding import PartitionSpec as P

ITERS = 3
BLOCKS = 4
F32 = jnp.float32
BF16 = jnp.bfloat16
NT = (((1,), (1,)), ((), ()))
NN = (((1,), (0,)), ((), ()))

CHUNKS = (
    ((0, 3), (1, 3), (2, 3), (3, 3), (0, 0)),
    ((0, 2), (1, 2), (2, 2), (0, 1), (1, 1)),
)


def split(value):
    high = value.astype(BF16)
    low = (value - high.astype(F32)).astype(BF16)
    return high, low


def split3(value):
    high = value.astype(BF16)
    return high, split(value - high.astype(F32))


def mm(left, right, dims):
    return lax.dot_general(left, right, dims, preferred_element_type=F32)


def units(chunk, bs):
    for i, j in chunk:
        yield i, j, 0, (bs // 2 if i == j else bs)
        yield i, j, 1, bs


def packed_rows(chunk, bs):
    return sum(rows for *_, rows in units(chunk, bs))


def pieces(chunk, bs):
    middle = packed_rows(chunk, bs) // 2
    base = 0
    for i, j, side, height in units(chunk, bs):
        cut = min(max(middle - base, 0), height)
        for lo, hi in ((0, cut), (cut, height)):
            if lo < hi:
                part = int(base + lo >= middle)
                first = base + lo - part * middle
                rows = slice(i * bs + lo, i * bs + hi)
                cols = slice(j * bs + side * (bs // 2), j * bs + (side + 1) * (bs // 2))
                yield part, slice(first, first + hi - lo), i == j and side, rows, cols
        base += height


def gram_kernel(bs, widths, u_hbm, *refs):
    count = len(CHUNKS)
    outs = refs[: 2 * count]
    u_ref, parts_ref, acc_ref, cross_ref, sems = refs[2 * count :]
    copies = []
    first = 0
    for number, width in enumerate(widths):
        cols = slice(first, first + width)
        copies.append(pltpu.make_async_copy(u_hbm.at[:, cols], u_ref.at[:, cols], sems.at[number]))
        copies[-1].start()
        first += width

    def add(ref, place, value, new):
        ref[place] = value if new else ref[place] + value

    first = 0
    for number, width in enumerate(widths):
        copies[number].wait()
        for j in range(BLOCKS):
            rows = slice(j * bs, (j + 1) * bs)
            high, low = split(u_ref[rows, first : first + width])
            for place, value in enumerate((high, high, low, high)):
                parts_ref[rows, place * width : (place + 1) * width] = value
        first += width
        for j in range(BLOCKS):
            above, end = j * bs, (j + 1) * bs
            if j:
                value = mm(
                    parts_ref[:above, width : 4 * width], parts_ref[above:end, : 3 * width], NT
                )
                add(acc_ref, (slice(0, above), slice(above, end)), value, number == 0)
            high = parts_ref[above:end, :width]
            low = parts_ref[above:end, 2 * width : 3 * width]
            own = (slice(above, end), slice(above, end))
            add(acc_ref, own, mm(high, high, NT), number == 0)
            add(cross_ref, j, mm(high, low, NT), number == 0)

    core = lax.rem(lax.axis_index("in"), 2)
    for j in range(BLOCKS):
        above, end = j * bs, (j + 1) * bs
        acc_ref[above:end, above:end] += cross_ref[j] + cross_ref[j].T
    for mine in range(2):

        @pl.when(core == mine)
        def _():
            for number, chunk in enumerate(CHUNKS):
                sent, kept = outs[2 * number : 2 * number + 2]
                for part, place, _, rows, cols in pieces(chunk, bs):
                    (kept if part == mine else sent)[place, :] = acc_ref[rows, cols]


def gram(unfolding):
    order, depth = unfolding.shape
    bs = order // BLOCKS
    widths = (depth // 8, depth // 4, 3 * depth // 8, depth // 4)
    heights = [packed_rows(chunk, bs) for chunk in CHUNKS]
    halves = [(height // 2, bs // 2) for height in heights for _ in range(2)]
    return pl.pallas_call(
        functools.partial(gram_kernel, bs, widths),
        in_specs=[pl.BlockSpec(memory_space=pl.ANY)],
        out_specs=[pl.BlockSpec(memory_space=pltpu.VMEM)] * len(halves),
        out_shape=[pltpu.VMEM(shape, F32) for shape in halves],
        scratch_shapes=[
            pltpu.VMEM((order, depth), F32),
            pltpu.VMEM((order, 4 * max(widths)), BF16),
            pltpu.VMEM((order, order), F32),
            pltpu.VMEM((BLOCKS, bs, bs), F32),
            pltpu.SemaphoreType.DMA((len(widths),)),
        ],
        compiler_params=pltpu.CompilerParams(vmem_limit_bytes=50 * 1024 * 1024),
        name="gram",
    )(unfolding)


def inverse_cholesky(inner):
    order = inner.shape[0]
    size = min(16, order)
    shape = (8, order)
    lane = lax.broadcasted_iota(jnp.int32, shape, 1)
    sub = lax.broadcasted_iota(jnp.int32, shape, 0)

    def lanes(value, k):
        return jnp.broadcast_to(value[:, k : k + 1], shape)

    def subs(value, i):
        return jnp.broadcast_to(value[i : i + 1, :], shape)

    def reciprocal(value):
        guess = pl.reciprocal(value, approx=True)
        return guess * (2.0 - value * guess)

    rows = [inner[m : m + 8, :] for m in range(0, order, 8)]
    result = []
    for first in range(0, order, size):
        inside = (lane >= first) & (lane < first + size)
        own = rows[first // 8 : (first + size) // 8]
        s = [[None] * (i + 1) for i in range(size)]
        for k in range(size):
            for g in range(k // 8, size // 8):
                column = lanes(own[g], first + k)
                for i in range(max(k, 8 * g), 8 * g + 8):
                    s[i][k] = subs(column, i - 8 * g)
        y = []
        for g in range(size // 8):
            unit = jnp.where(lane == first + 8 * g + sub, 1.0, 0.0)
            masked = jnp.where(inside, unit, own[g])
            y += [subs(masked, i) for i in range(8)]
        inverse = [None] * size
        f = [[None] * size for _ in range(size)]
        for k in range(size):
            inverse[k] = reciprocal(s[k][k])
            for i in range(k + 1, size):
                f[i][k] = s[i][k] * inverse[k]
            for i in range(k + 1, size):
                for j in range(k + 1, i + 1):
                    s[i][j] = s[i][j] - f[i][k] * s[j][k]
                y[i] = y[i] - f[i][k] * y[k]
        p = [y[k] * inverse[k] for k in range(size)]
        for j in range(size - 1, 0, -1):
            for i in range(j - 1, -1, -1):
                p[i] = p[i] - f[j][i] * p[j]
        for g in range(size // 8):
            out = y[8 * g] * lax.rsqrt(s[8 * g][8 * g])
            for i in range(1, 8):
                out = jnp.where(sub == i, y[8 * g + i] * lax.rsqrt(s[8 * g + i][8 * g + i]), out)
            result.append(jnp.where(lane <= first + 8 * g + sub, out, 0.0))
        for m in range((first + size) // 8, order // 8):
            value = jnp.where(inside, 0.0, rows[m])
            for k in range(size - 1, -1, -1):
                value = value - lanes(rows[m], first + k) * p[k]
            rows[m] = value
    return jnp.concatenate(result, axis=0)


def iterate_kernel(bs, start_hbm, *refs):
    count = 2 * len(CHUNKS)
    halves, refs = refs[:count], refs[count:]
    u_hbm, factor_hbm, core_hbm, *refs = refs
    g_high, g_low, both_ref, basis, parts_ref, u_vmem, factor_ref, core_ref, sems, out_sem = refs
    rank = basis.shape[0]
    half = bs // 2
    start_copy = pltpu.make_async_copy(start_hbm, factor_ref, sems.at[0])
    start_copy.start()
    copy = pltpu.make_async_copy(u_hbm, u_vmem, sems.at[1])
    copy.start()
    core = lax.rem(lax.axis_index("in"), 2)
    for mine in range(2):

        @pl.when(core == mine)
        def _():
            for number, chunk in enumerate(CHUNKS):
                own, other = halves[2 * number : 2 * number + 2]
                for part, place, lower, rows, cols in pieces(chunk, bs):
                    value = (own if part == mine else other)[place, :]
                    g_high[rows, cols], g_low[rows, cols] = split(value)
                    if lower and rows.start % bs == 0:
                        below = (slice(rows.start + half, rows.start + bs), slice(cols.start - half, cols.start))
                        g_high[below], g_low[below] = split(value[:half].T)

    start_copy.wait()
    high, low = split(factor_ref[...].T)
    both_ref[:rank, :] = high
    both_ref[rank:, :] = low

    def body(_, carry):
        for j in range(BLOCKS):
            above, end = j * bs, (j + 1) * bs
            total = mm(both_ref[:, :end], g_high[:end, above:end], NN)
            extra = mm(both_ref[:rank, :end], g_low[:end, above:end], NN)
            if j < BLOCKS - 1:
                total += mm(both_ref[:, end:], g_high[above:end, end:], NT)
                extra += mm(both_ref[:rank, end:], g_low[above:end, end:], NT)
            value = total[:rank] + (total[rank:] + extra)
            high, rest = split3(value)
            parts_ref[:rank, above:end] = rest[0]
            parts_ref[rank : 2 * rank, above:end] = high
            parts_ref[2 * rank :, above:end] = rest[1]
        product = mm(parts_ref[...], parts_ref[: 2 * rank, :], NT)
        cross = product[2 * rank :, rank:]
        inner = product[rank : 2 * rank, rank:] + (
            (product[:rank, rank:] + product[rank : 2 * rank, :rank])
            + (product[:rank, :rank] + (cross + cross.T))
        )
        high, (middle, low) = split3(inverse_cholesky(inner))
        left = jnp.concatenate(
            [
                jnp.concatenate([middle, high], axis=1),
                jnp.concatenate([high, middle], axis=1),
            ],
            axis=0,
        )
        last = jnp.concatenate([low, high], axis=1)
        for j in range(BLOCKS):
            cols = slice(j * bs, (j + 1) * bs)
            product = mm(left, parts_ref[: 2 * rank, cols], NN)
            product = product[:rank] + (product[rank:] + mm(last, parts_ref[rank:, cols], NN))
            basis[:, cols] = product
            both_ref[:rank, cols], both_ref[rank:, cols] = split(product)
        return carry

    lax.fori_loop(0, ITERS, body, 0)
    factor_ref[...] = basis[...].T
    depth = u_vmem.shape[1]
    step = min(512, depth)
    outs = [pltpu.make_async_copy(factor_ref, factor_hbm, out_sem.at[0])]
    outs[0].start()
    copy.wait()
    for number, lo in enumerate(range(0, depth, step)):
        cols = slice(lo, lo + step)
        u_high, u_low = split(u_vmem[:, cols])
        total = mm(both_ref[...], u_high, NN)
        core_ref[:, cols] = total[:rank] + (total[rank:] + mm(both_ref[:rank, :], u_low, NN))
        outs.append(
            pltpu.make_async_copy(core_ref.at[:, cols], core_hbm.at[:, cols], out_sem.at[number + 1])
        )
        outs[-1].start()
    for out in outs:
        out.wait()


def iterate(start, halves, unfolding):
    order, rank = start.shape
    depth = unfolding.shape[1]
    bs = order // BLOCKS
    vmem = pl.BlockSpec(memory_space=pltpu.VMEM)
    hbm = pl.BlockSpec(memory_space=pl.ANY)
    return pl.pallas_call(
        functools.partial(iterate_kernel, bs),
        in_specs=[hbm] + [vmem] * len(halves) + [hbm],
        out_specs=[hbm, hbm],
        out_shape=[
            jax.ShapeDtypeStruct((order, rank), F32),
            jax.ShapeDtypeStruct((rank, depth), F32),
        ],
        scratch_shapes=[
            pltpu.VMEM((order, order), BF16),
            pltpu.VMEM((order, order), BF16),
            pltpu.VMEM((2 * rank, order), BF16),
            pltpu.VMEM((rank, order), F32),
            pltpu.VMEM((3 * rank, order), BF16),
            pltpu.VMEM((order, depth), F32),
            pltpu.VMEM((order, rank), F32),
            pltpu.VMEM((rank, depth), F32),
            pltpu.SemaphoreType.DMA((2,)),
            pltpu.SemaphoreType.DMA((1 + depth // min(512, depth),)),
        ],
        compiler_params=pltpu.CompilerParams(vmem_limit_bytes=36 * 1024 * 1024),
        name="iterate",
    )(start, *halves, unfolding)


class Exchange:
    def __init__(self, groups, inner, inner_first):
        self.groups, self.inner = groups, inner
        grp = [("grp", k) for k in range(groups.bit_length() - 1)]
        rest = [("in", k) for k in range(1, inner.bit_length() - 1)]
        before, after = (rest[:1], rest[1:]) if inner_first else ([], rest)
        self.orders = tuple(before + g + after for g in (grp, grp[:2][::-1] + grp[2:]))
        self.index = {"grp": lax.axis_index("grp"), "in": lax.axis_index("in")}
        self.core = self.index["in"] & 1

    def swap(self, value, stage):
        pairs = []
        for g in range(self.groups):
            for i in range(self.inner):
                axis, bit = ("in", 0) if stage is None else self.orders[i & 1][stage]
                to = (g ^ (1 << bit), i) if axis == "grp" else (g, i ^ (1 << bit))
                pairs.append((g * self.inner + i, to[0] * self.inner + to[1]))
        return lax.ppermute(value, ("grp", "in"), pairs)

    def bit(self, stage):
        bits = [(self.index[axis] >> k) & 1 for axis, k in (order[stage] for order in self.orders)]
        return jnp.where(self.core == 0, bits[0], bits[1])

    def all_sum(self, sent, kept):
        last = len(self.orders[0]) - 1
        came = self.swap(sent, None)
        for stage in range(last):
            bit = self.bit(stage)
            parts = [x.reshape(2, x.shape[0] // 2, x.shape[1]) for x in (kept, came)]

            def half(place):
                own, new = (lax.dynamic_index_in_dim(x, place, 0, keepdims=False) for x in parts)
                return own + new

            sent, kept = half(1 - bit), half(bit)
            came = self.swap(sent, stage)
        value = kept + came
        value = value + self.swap(value, last)
        for stage in range(last - 1, -1, -1):
            came = self.swap(value, stage)
            bit = self.bit(stage)
            whole = jnp.zeros((2,) + value.shape, value.dtype)
            whole = lax.dynamic_update_index_in_dim(whole, value, bit, 0)
            whole = lax.dynamic_update_index_in_dim(whole, came, 1 - bit, 0)
            value = whole.reshape(-1, value.shape[1])
        return value, self.swap(value, None)


def per_device(groups, inner, unfolding, start_basis):
    parts = gram(unfolding)
    halves = []
    for number in range(len(CHUNKS)):
        exchange = Exchange(groups, inner, number > 0)
        halves += exchange.all_sum(*parts[2 * number : 2 * number + 2])
    factor, core_block = iterate(start_basis, halves, unfolding)
    return (factor, core_block)


def solution(mesh):
    in_specs = (P(None, ("grp", "in")), P())
    out_specs = (P(), P(None, ("grp", "in")))
    body = functools.partial(per_device, mesh.shape["grp"], mesh.shape["in"])
    return jax.shard_map(body, mesh=mesh, in_specs=in_specs, out_specs=out_specs, check_vma=False)
```

```python
import functools

import jax
import jax.numpy as jnp
from jax import lax
from jax.experimental import pallas as pl
from jax.experimental.pallas import tpu as pltpu
from jax.sharding import PartitionSpec as P

ITERS = 3
BLOCKS = 4
F32 = jnp.float32
BF16 = jnp.bfloat16
NT = (((1,), (1,)), ((), ()))
NN = (((1,), (0,)), ((), ()))

CHUNKS = (
    ((0, 3), (1, 3), (2, 3), (3, 3), (0, 0)),
    ((0, 2), (1, 2), (2, 2), (0, 1), (1, 1)),
)


def split(value):
    high = value.astype(BF16)
    low = (value - high.astype(F32)).astype(BF16)
    return high, low


def split3(value):
    high = value.astype(BF16)
    return high, split(value - high.astype(F32))


def mm(left, right, dims):
    return lax.dot_general(left, right, dims, preferred_element_type=F32)


def units(chunk, bs):
    for i, j in chunk:
        yield i, j, 0, (bs // 2 if i == j else bs)
        yield i, j, 1, bs


def packed_rows(chunk, bs):
    return sum(rows for *_, rows in units(chunk, bs))


def pieces(chunk, bs):
    middle = packed_rows(chunk, bs) // 2
    base = 0
    for i, j, side, height in units(chunk, bs):
        cut = min(max(middle - base, 0), height)
        for lo, hi in ((0, cut), (cut, height)):
            if lo < hi:
                part = int(base + lo >= middle)
                first = base + lo - part * middle
                rows = slice(i * bs + lo, i * bs + hi)
                cols = slice(j * bs + side * (bs // 2), j * bs + (side + 1) * (bs // 2))
                yield part, slice(first, first + hi - lo), i == j and side, rows, cols
        base += height


def gram_kernel(bs, u_hbm, *refs):
    outs = refs[: 2 * len(CHUNKS)]
    u_ref, parts_ref, acc_ref, cross_ref, sems = refs[2 * len(CHUNKS) :]
    steps, _, width = u_ref.shape

    def copy(step):
        cols = pl.ds(pl.multiple_of(step * width, width), width)
        return pltpu.make_async_copy(u_hbm.at[:, cols], u_ref.at[step], sems.at[step])

    for step in range(steps):
        copy(step).start()
    acc_ref[...] = jnp.zeros_like(acc_ref)
    cross_ref[...] = jnp.zeros_like(cross_ref)

    def body(step, carry):
        copy(step).wait()
        for j in range(BLOCKS):
            rows = slice(j * bs, (j + 1) * bs)
            high, low = split(u_ref[step, rows, :])
            for place, value in enumerate((high, high, low, high)):
                parts_ref[rows, place * width : (place + 1) * width] = value
        for j in range(BLOCKS):
            above, end = j * bs, (j + 1) * bs
            if j:
                acc_ref[:above, above:end] += mm(
                    parts_ref[:above, width : 4 * width], parts_ref[above:end, : 3 * width], NT
                )
            high = parts_ref[above:end, :width]
            acc_ref[above:end, above:end] += mm(high, high, NT)
            cross_ref[j] += mm(high, parts_ref[above:end, 2 * width : 3 * width], NT)
        return carry

    lax.fori_loop(0, steps, body, 0)
    core = lax.rem(lax.axis_index("in"), 2)
    for j in range(BLOCKS):
        above, end = j * bs, (j + 1) * bs
        acc_ref[above:end, above:end] += cross_ref[j] + cross_ref[j].T
    for mine in range(2):

        @pl.when(core == mine)
        def _():
            for number, chunk in enumerate(CHUNKS):
                sent, kept = outs[2 * number : 2 * number + 2]
                for part, place, _, rows, cols in pieces(chunk, bs):
                    (kept if part == mine else sent)[place, :] = acc_ref[rows, cols]


def gram(unfolding):
    order, depth = unfolding.shape
    bs = order // BLOCKS
    steps = 4
    width = depth // steps
    heights = [packed_rows(chunk, bs) for chunk in CHUNKS]
    halves = [(height // 2, bs // 2) for height in heights for _ in range(2)]
    return pl.pallas_call(
        functools.partial(gram_kernel, bs),
        in_specs=[pl.BlockSpec(memory_space=pl.ANY)],
        out_specs=[pl.BlockSpec(memory_space=pltpu.VMEM)] * len(halves),
        out_shape=[pltpu.VMEM(shape, F32) for shape in halves],
        scratch_shapes=[
            pltpu.VMEM((steps, order, width), F32),
            pltpu.VMEM((order, 4 * width), BF16),
            pltpu.VMEM((order, order), F32),
            pltpu.VMEM((BLOCKS, bs, bs), F32),
            pltpu.SemaphoreType.DMA((steps,)),
        ],
        compiler_params=pltpu.CompilerParams(vmem_limit_bytes=50 * 1024 * 1024),
        name="gram",
    )(unfolding)


def inverse_cholesky(inner):
    order = inner.shape[0]
    size = min(16, order)
    shape = (8, order)
    lane = lax.broadcasted_iota(jnp.int32, shape, 1)
    sub = lax.broadcasted_iota(jnp.int32, shape, 0)

    def lanes(value, k):
        return jnp.broadcast_to(value[:, k : k + 1], shape)

    def subs(value, i):
        return jnp.broadcast_to(value[i : i + 1, :], shape)

    def reciprocal(value):
        guess = pl.reciprocal(value, approx=True)
        return guess * (2.0 - value * guess)

    rows = [inner[m : m + 8, :] for m in range(0, order, 8)]
    result = []
    for first in range(0, order, size):
        inside = (lane >= first) & (lane < first + size)
        own = rows[first // 8 : (first + size) // 8]
        s = [[None] * (i + 1) for i in range(size)]
        for k in range(size):
            for g in range(k // 8, size // 8):
                column = lanes(own[g], first + k)
                for i in range(max(k, 8 * g), 8 * g + 8):
                    s[i][k] = subs(column, i - 8 * g)
        y = []
        for g in range(size // 8):
            unit = jnp.where(lane == first + 8 * g + sub, 1.0, 0.0)
            masked = jnp.where(inside, unit, own[g])
            y += [subs(masked, i) for i in range(8)]
        inverse = [None] * size
        f = [[None] * size for _ in range(size)]
        for k in range(size):
            inverse[k] = reciprocal(s[k][k])
            for i in range(k + 1, size):
                f[i][k] = s[i][k] * inverse[k]
            for i in range(k + 1, size):
                for j in range(k + 1, i + 1):
                    s[i][j] = s[i][j] - f[i][k] * s[j][k]
                y[i] = y[i] - f[i][k] * y[k]
        p = [y[k] * inverse[k] for k in range(size)]
        for j in range(size - 1, 0, -1):
            for i in range(j - 1, -1, -1):
                p[i] = p[i] - f[j][i] * p[j]
        for g in range(size // 8):
            out = y[8 * g] * lax.rsqrt(s[8 * g][8 * g])
            for i in range(1, 8):
                out = jnp.where(sub == i, y[8 * g + i] * lax.rsqrt(s[8 * g + i][8 * g + i]), out)
            result.append(jnp.where(lane <= first + 8 * g + sub, out, 0.0))
        for m in range((first + size) // 8, order // 8):
            value = jnp.where(inside, 0.0, rows[m])
            for k in range(size - 1, -1, -1):
                value = value - lanes(rows[m], first + k) * p[k]
            rows[m] = value
    return jnp.concatenate(result, axis=0)


def iterate_kernel(bs, start_hbm, *refs):
    count = 2 * len(CHUNKS)
    halves, refs = refs[:count], refs[count:]
    u_hbm, factor_hbm, core_hbm, *refs = refs
    g_high, g_low, both_ref, basis, parts_ref, u_vmem, factor_ref, core_ref, sems, out_sem = refs
    rank = basis.shape[0]
    half = bs // 2
    start_copy = pltpu.make_async_copy(start_hbm, factor_ref, sems.at[0])
    start_copy.start()
    copy = pltpu.make_async_copy(u_hbm, u_vmem, sems.at[1])
    copy.start()
    core = lax.rem(lax.axis_index("in"), 2)
    for mine in range(2):

        @pl.when(core == mine)
        def _():
            for number, chunk in enumerate(CHUNKS):
                own, other = halves[2 * number : 2 * number + 2]
                for part, place, lower, rows, cols in pieces(chunk, bs):
                    value = (own if part == mine else other)[place, :]
                    g_high[rows, cols], g_low[rows, cols] = split(value)
                    if lower and rows.start % bs == 0:
                        below = (slice(rows.start + half, rows.start + bs), slice(cols.start - half, cols.start))
                        g_high[below], g_low[below] = split(value[:half].T)

    start_copy.wait()
    high, low = split(factor_ref[...].T)
    both_ref[:rank, :] = high
    both_ref[rank:, :] = low

    def body(_, carry):
        for j in range(BLOCKS):
            above, end = j * bs, (j + 1) * bs
            total = mm(both_ref[:, :end], g_high[:end, above:end], NN)
            extra = mm(both_ref[:rank, :end], g_low[:end, above:end], NN)
            if j < BLOCKS - 1:
                total += mm(both_ref[:, end:], g_high[above:end, end:], NT)
                extra += mm(both_ref[:rank, end:], g_low[above:end, end:], NT)
            value = total[:rank] + (total[rank:] + extra)
            high, rest = split3(value)
            parts_ref[:rank, above:end] = rest[0]
            parts_ref[rank : 2 * rank, above:end] = high
            parts_ref[2 * rank :, above:end] = rest[1]
        product = mm(parts_ref[...], parts_ref[: 2 * rank, :], NT)
        cross = product[2 * rank :, rank:]
        inner = product[rank : 2 * rank, rank:] + (
            (product[:rank, rank:] + product[rank : 2 * rank, :rank])
            + (product[:rank, :rank] + (cross + cross.T))
        )
        high, (middle, low) = split3(inverse_cholesky(inner))
        left = jnp.concatenate(
            [
                jnp.concatenate([middle, high], axis=1),
                jnp.concatenate([high, middle], axis=1),
            ],
            axis=0,
        )
        last = jnp.concatenate([low, high], axis=1)
        for j in range(BLOCKS):
            cols = slice(j * bs, (j + 1) * bs)
            product = mm(left, parts_ref[: 2 * rank, cols], NN)
            product = product[:rank] + (product[rank:] + mm(last, parts_ref[rank:, cols], NN))
            basis[:, cols] = product
            both_ref[:rank, cols], both_ref[rank:, cols] = split(product)
        return carry

    lax.fori_loop(0, ITERS, body, 0)
    factor_ref[...] = basis[...].T
    depth = u_vmem.shape[1]
    step = min(512, depth)
    outs = [pltpu.make_async_copy(factor_ref, factor_hbm, out_sem.at[0])]
    outs[0].start()
    copy.wait()
    for number, lo in enumerate(range(0, depth, step)):
        cols = slice(lo, lo + step)
        u_high, u_low = split(u_vmem[:, cols])
        total = mm(both_ref[...], u_high, NN)
        core_ref[:, cols] = total[:rank] + (total[rank:] + mm(both_ref[:rank, :], u_low, NN))
        outs.append(
            pltpu.make_async_copy(core_ref.at[:, cols], core_hbm.at[:, cols], out_sem.at[number + 1])
        )
        outs[-1].start()
    for out in outs:
        out.wait()


def iterate(start, halves, unfolding):
    order, rank = start.shape
    depth = unfolding.shape[1]
    bs = order // BLOCKS
    vmem = pl.BlockSpec(memory_space=pltpu.VMEM)
    hbm = pl.BlockSpec(memory_space=pl.ANY)
    return pl.pallas_call(
        functools.partial(iterate_kernel, bs),
        in_specs=[hbm] + [vmem] * len(halves) + [hbm],
        out_specs=[hbm, hbm],
        out_shape=[
            jax.ShapeDtypeStruct((order, rank), F32),
            jax.ShapeDtypeStruct((rank, depth), F32),
        ],
        scratch_shapes=[
            pltpu.VMEM((order, order), BF16),
            pltpu.VMEM((order, order), BF16),
            pltpu.VMEM((2 * rank, order), BF16),
            pltpu.VMEM((rank, order), F32),
            pltpu.VMEM((3 * rank, order), BF16),
            pltpu.VMEM((order, depth), F32),
            pltpu.VMEM((order, rank), F32),
            pltpu.VMEM((rank, depth), F32),
            pltpu.SemaphoreType.DMA((2,)),
            pltpu.SemaphoreType.DMA((1 + depth // min(512, depth),)),
        ],
        compiler_params=pltpu.CompilerParams(vmem_limit_bytes=36 * 1024 * 1024),
        name="iterate",
    )(start, *halves, unfolding)


class Exchange:
    def __init__(self, groups, inner, inner_first):
        self.groups, self.inner = groups, inner
        grp = [("grp", k) for k in range(groups.bit_length() - 1)]
        rest = [("in", k) for k in range(1, inner.bit_length() - 1)]
        before, after = (rest[:1], rest[1:]) if inner_first else ([], rest)
        self.orders = tuple(before + g + after for g in (grp, grp[:2][::-1] + grp[2:]))
        self.index = {"grp": lax.axis_index("grp"), "in": lax.axis_index("in")}
        self.core = self.index["in"] & 1

    def swap(self, value, stage):
        pairs = []
        for g in range(self.groups):
            for i in range(self.inner):
                axis, bit = ("in", 0) if stage is None else self.orders[i & 1][stage]
                to = (g ^ (1 << bit), i) if axis == "grp" else (g, i ^ (1 << bit))
                pairs.append((g * self.inner + i, to[0] * self.inner + to[1]))
        return lax.ppermute(value, ("grp", "in"), pairs)

    def bit(self, stage):
        bits = [(self.index[axis] >> k) & 1 for axis, k in (order[stage] for order in self.orders)]
        return jnp.where(self.core == 0, bits[0], bits[1])

    def all_sum(self, sent, kept):
        last = len(self.orders[0]) - 1
        came = self.swap(sent, None)
        for stage in range(last):
            bit = self.bit(stage)
            parts = [x.reshape(2, x.shape[0] // 2, x.shape[1]) for x in (kept, came)]

            def half(place):
                own, new = (lax.dynamic_index_in_dim(x, place, 0, keepdims=False) for x in parts)
                return own + new

            sent, kept = half(1 - bit), half(bit)
            came = self.swap(sent, stage)
        value = kept + came
        value = value + self.swap(value, last)
        for stage in range(last - 1, -1, -1):
            came = self.swap(value, stage)
            bit = self.bit(stage)
            whole = jnp.zeros((2,) + value.shape, value.dtype)
            whole = lax.dynamic_update_index_in_dim(whole, value, bit, 0)
            whole = lax.dynamic_update_index_in_dim(whole, came, 1 - bit, 0)
            value = whole.reshape(-1, value.shape[1])
        return value, self.swap(value, None)


def per_device(groups, inner, unfolding, start_basis):
    parts = gram(unfolding)
    halves = []
    for number in range(len(CHUNKS)):
        exchange = Exchange(groups, inner, number == 0)
        halves += exchange.all_sum(*parts[2 * number : 2 * number + 2])
    factor, core_block = iterate(start_basis, halves, unfolding)
    return (factor, core_block)


def solution(mesh):
    in_specs = (P(None, ("grp", "in")), P())
    out_specs = (P(), P(None, ("grp", "in")))
    body = functools.partial(per_device, mesh.shape["grp"], mesh.shape["in"])
    return jax.shard_map(body, mesh=mesh, in_specs=in_specs, out_specs=out_specs, check_vma=False)
```

```python
import functools

import jax
import jax.numpy as jnp
from jax import lax
from jax.experimental import pallas as pl
from jax.experimental.pallas import tpu as pltpu
from jax.sharding import PartitionSpec as P

ITERS = 3
BLOCKS = 4
F32 = jnp.float32
BF16 = jnp.bfloat16
NT = (((1,), (1,)), ((), ()))
NN = (((1,), (0,)), ((), ()))

CHUNKS = (
    ((0, 3), (1, 3), (2, 3), (3, 3), (0, 0)),
    ((0, 2), (1, 2), (2, 2), (0, 1), (1, 1)),
)


def split(value):
    high = value.astype(BF16)
    low = (value - high.astype(F32)).astype(BF16)
    return high, low


def split3(value):
    high = value.astype(BF16)
    return high, split(value - high.astype(F32))


def mm(left, right, dims):
    return lax.dot_general(left, right, dims, preferred_element_type=F32)


def units(chunk, bs):
    for i, j in chunk:
        yield i, j, 0, (bs // 2 if i == j else bs)
        yield i, j, 1, bs


def packed_rows(chunk, bs):
    return sum(rows for *_, rows in units(chunk, bs))


def pieces(chunk, bs):
    middle = packed_rows(chunk, bs) // 2
    base = 0
    for i, j, side, height in units(chunk, bs):
        cut = min(max(middle - base, 0), height)
        for lo, hi in ((0, cut), (cut, height)):
            if lo < hi:
                part = int(base + lo >= middle)
                first = base + lo - part * middle
                rows = slice(i * bs + lo, i * bs + hi)
                cols = slice(j * bs + side * (bs // 2), j * bs + (side + 1) * (bs // 2))
                yield part, slice(first, first + hi - lo), i == j and side, rows, cols
        base += height


def gram_kernel(bs, u_hbm, *refs):
    outs = refs[: 2 * len(CHUNKS)]
    u_ref, parts_ref, acc_ref, cross_ref, sems = refs[2 * len(CHUNKS) :]
    steps, _, width = u_ref.shape

    def copy(step):
        cols = pl.ds(pl.multiple_of(step * width, width), width)
        return pltpu.make_async_copy(u_hbm.at[:, cols], u_ref.at[step], sems.at[step])

    for step in range(steps):
        copy(step).start()
    acc_ref[...] = jnp.zeros_like(acc_ref)
    cross_ref[...] = jnp.zeros_like(cross_ref)

    def body(step, carry):
        copy(step).wait()
        for j in range(BLOCKS):
            rows = slice(j * bs, (j + 1) * bs)
            high, low = split(u_ref[step, rows, :])
            for place, value in enumerate((high, high, low, high)):
                parts_ref[rows, place * width : (place + 1) * width] = value
        for j in range(BLOCKS):
            above, end = j * bs, (j + 1) * bs
            if j:
                acc_ref[:above, above:end] += mm(
                    parts_ref[:above, width : 4 * width], parts_ref[above:end, : 3 * width], NT
                )
            high = parts_ref[above:end, :width]
            acc_ref[above:end, above:end] += mm(high, high, NT)
            cross_ref[j] += mm(high, parts_ref[above:end, 2 * width : 3 * width], NT)
        return carry

    lax.fori_loop(0, steps, body, 0)
    core = lax.rem(lax.axis_index("in"), 2)
    for j in range(BLOCKS):
        above, end = j * bs, (j + 1) * bs
        acc_ref[above:end, above:end] += cross_ref[j] + cross_ref[j].T
    for mine in range(2):

        @pl.when(core == mine)
        def _():
            for number, chunk in enumerate(CHUNKS):
                sent, kept = outs[2 * number : 2 * number + 2]
                for part, place, _, rows, cols in pieces(chunk, bs):
                    (kept if part == mine else sent)[place, :] = acc_ref[rows, cols]


def gram(unfolding):
    order, depth = unfolding.shape
    bs = order // BLOCKS
    steps = 4
    width = depth // steps
    heights = [packed_rows(chunk, bs) for chunk in CHUNKS]
    halves = [(height // 2, bs // 2) for height in heights for _ in range(2)]
    return pl.pallas_call(
        functools.partial(gram_kernel, bs),
        in_specs=[pl.BlockSpec(memory_space=pl.ANY)],
        out_specs=[pl.BlockSpec(memory_space=pltpu.VMEM)] * len(halves),
        out_shape=[pltpu.VMEM(shape, F32) for shape in halves],
        scratch_shapes=[
            pltpu.VMEM((steps, order, width), F32),
            pltpu.VMEM((order, 4 * width), BF16),
            pltpu.VMEM((order, order), F32),
            pltpu.VMEM((BLOCKS, bs, bs), F32),
            pltpu.SemaphoreType.DMA((steps,)),
        ],
        compiler_params=pltpu.CompilerParams(vmem_limit_bytes=50 * 1024 * 1024),
        name="gram",
    )(unfolding)


def inverse_cholesky(inner):
    order = inner.shape[0]
    size = min(16, order)
    shape = (8, order)
    lane = lax.broadcasted_iota(jnp.int32, shape, 1)
    sub = lax.broadcasted_iota(jnp.int32, shape, 0)

    def lanes(value, k):
        return jnp.broadcast_to(value[:, k : k + 1], shape)

    def subs(value, i):
        return jnp.broadcast_to(value[i : i + 1, :], shape)

    def reciprocal(value):
        guess = pl.reciprocal(value, approx=True)
        return guess * (2.0 - value * guess)

    rows = [inner[m : m + 8, :] for m in range(0, order, 8)]
    result = []
    for first in range(0, order, size):
        inside = (lane >= first) & (lane < first + size)
        own = rows[first // 8 : (first + size) // 8]
        s = [[None] * (i + 1) for i in range(size)]
        for k in range(size):
            for g in range(k // 8, size // 8):
                column = lanes(own[g], first + k)
                for i in range(max(k, 8 * g), 8 * g + 8):
                    s[i][k] = subs(column, i - 8 * g)
        y = []
        for g in range(size // 8):
            unit = jnp.where(lane == first + 8 * g + sub, 1.0, 0.0)
            masked = jnp.where(inside, unit, own[g])
            y += [subs(masked, i) for i in range(8)]
        inverse = [None] * size
        f = [[None] * size for _ in range(size)]
        for k in range(size):
            inverse[k] = reciprocal(s[k][k])
            for i in range(k + 1, size):
                f[i][k] = s[i][k] * inverse[k]
            for i in range(k + 1, size):
                for j in range(k + 1, i + 1):
                    s[i][j] = s[i][j] - f[i][k] * s[j][k]
                y[i] = y[i] - f[i][k] * y[k]
        p = [y[k] * inverse[k] for k in range(size)]
        for j in range(size - 1, 0, -1):
            for i in range(j - 1, -1, -1):
                p[i] = p[i] - f[j][i] * p[j]
        for g in range(size // 8):
            out = y[8 * g] * lax.rsqrt(s[8 * g][8 * g])
            for i in range(1, 8):
                out = jnp.where(sub == i, y[8 * g + i] * lax.rsqrt(s[8 * g + i][8 * g + i]), out)
            result.append(jnp.where(lane <= first + 8 * g + sub, out, 0.0))
        for m in range((first + size) // 8, order // 8):
            value = jnp.where(inside, 0.0, rows[m])
            for k in range(size - 1, -1, -1):
                value = value - lanes(rows[m], first + k) * p[k]
            rows[m] = value
    return jnp.concatenate(result, axis=0)


def iterate_kernel(bs, start_hbm, *refs):
    count = 2 * len(CHUNKS)
    halves, refs = refs[:count], refs[count:]
    u_hbm, factor_hbm, core_hbm, *refs = refs
    g_high, g_low, both_ref, basis, parts_ref, u_vmem, factor_ref, core_ref, sems, out_sem = refs
    rank = basis.shape[0]
    half = bs // 2
    start_copy = pltpu.make_async_copy(start_hbm, factor_ref, sems.at[0])
    start_copy.start()
    copy = pltpu.make_async_copy(u_hbm, u_vmem, sems.at[1])
    copy.start()
    core = lax.rem(lax.axis_index("in"), 2)
    for mine in range(2):

        @pl.when(core == mine)
        def _():
            for number, chunk in enumerate(CHUNKS):
                own, other = halves[2 * number : 2 * number + 2]
                for part, place, lower, rows, cols in pieces(chunk, bs):
                    value = (own if part == mine else other)[place, :]
                    g_high[rows, cols], g_low[rows, cols] = split(value)
                    if lower and rows.start % bs == 0:
                        below = (slice(rows.start + half, rows.start + bs), slice(cols.start - half, cols.start))
                        g_high[below], g_low[below] = split(value[:half].T)

    start_copy.wait()
    high, low = split(factor_ref[...].T)
    both_ref[:rank, :] = high
    both_ref[rank:, :] = low

    def body(_, carry):
        for j in range(BLOCKS):
            above, end = j * bs, (j + 1) * bs
            total = mm(both_ref[:, :end], g_high[:end, above:end], NN)
            extra = mm(both_ref[:rank, :end], g_low[:end, above:end], NN)
            if j < BLOCKS - 1:
                total += mm(both_ref[:, end:], g_high[above:end, end:], NT)
                extra += mm(both_ref[:rank, end:], g_low[above:end, end:], NT)
            value = total[:rank] + (total[rank:] + extra)
            high, rest = split3(value)
            parts_ref[:rank, above:end] = rest[0]
            parts_ref[rank : 2 * rank, above:end] = high
            parts_ref[2 * rank :, above:end] = rest[1]
        product = mm(parts_ref[...], parts_ref[: 2 * rank, :], NT)
        cross = product[2 * rank :, rank:]
        inner = product[rank : 2 * rank, rank:] + (
            (product[:rank, rank:] + product[rank : 2 * rank, :rank])
            + (product[:rank, :rank] + (cross + cross.T))
        )
        high, (middle, low) = split3(inverse_cholesky(inner))
        left = jnp.concatenate(
            [
                jnp.concatenate([middle, high], axis=1),
                jnp.concatenate([high, middle], axis=1),
            ],
            axis=0,
        )
        last = jnp.concatenate([low, high], axis=1)
        for j in range(BLOCKS):
            cols = slice(j * bs, (j + 1) * bs)
            product = mm(left, parts_ref[: 2 * rank, cols], NN)
            product = product[:rank] + (product[rank:] + mm(last, parts_ref[rank:, cols], NN))
            basis[:, cols] = product
            both_ref[:rank, cols], both_ref[rank:, cols] = split(product)
        return carry

    lax.fori_loop(0, ITERS, body, 0)
    factor_ref[...] = basis[...].T
    depth = u_vmem.shape[1]
    step = min(512, depth // 2)
    factor_copy = pltpu.make_async_copy(factor_ref, factor_hbm, out_sem.at[0])
    factor_copy.start()
    copy.wait()

    def out_copy(chunk):
        cols = pl.ds(pl.multiple_of(chunk * step, step), step)
        return pltpu.make_async_copy(core_ref.at[:, cols], core_hbm.at[:, cols], out_sem.at[1 + chunk])

    def pair(number, carry):
        for chunk in (2 * number, 2 * number + 1):
            cols = pl.ds(pl.multiple_of(chunk * step, step), step)
            u_high, u_low = split(u_vmem[:, cols])
            total = mm(both_ref[...], u_high, NN)
            core_ref[:, cols] = total[:rank] + (total[rank:] + mm(both_ref[:rank, :], u_low, NN))
            out_copy(chunk).start()
        return carry

    lax.fori_loop(0, depth // (2 * step), pair, 0)
    factor_copy.wait()
    for chunk in range(depth // step):
        out_copy(chunk).wait()


def iterate(start, halves, unfolding):
    order, rank = start.shape
    depth = unfolding.shape[1]
    bs = order // BLOCKS
    vmem = pl.BlockSpec(memory_space=pltpu.VMEM)
    hbm = pl.BlockSpec(memory_space=pl.ANY)
    return pl.pallas_call(
        functools.partial(iterate_kernel, bs),
        in_specs=[hbm] + [vmem] * len(halves) + [hbm],
        out_specs=[hbm, hbm],
        out_shape=[
            jax.ShapeDtypeStruct((order, rank), F32),
            jax.ShapeDtypeStruct((rank, depth), F32),
        ],
        scratch_shapes=[
            pltpu.VMEM((order, order), BF16),
            pltpu.VMEM((order, order), BF16),
            pltpu.VMEM((2 * rank, order), BF16),
            pltpu.VMEM((rank, order), F32),
            pltpu.VMEM((3 * rank, order), BF16),
            pltpu.VMEM((order, depth), F32),
            pltpu.VMEM((order, rank), F32),
            pltpu.VMEM((rank, depth), F32),
            pltpu.SemaphoreType.DMA((2,)),
            pltpu.SemaphoreType.DMA((1 + depth // min(512, depth // 2),)),
        ],
        compiler_params=pltpu.CompilerParams(vmem_limit_bytes=36 * 1024 * 1024),
        name="iterate",
    )(start, *halves, unfolding)


class Exchange:
    def __init__(self, groups, inner, inner_first):
        self.groups, self.inner = groups, inner
        grp = [("grp", k) for k in range(groups.bit_length() - 1)]
        rest = [("in", k) for k in range(1, inner.bit_length() - 1)]
        before, after = (rest[:1], rest[1:]) if inner_first else ([], rest)
        self.orders = tuple(before + g + after for g in (grp, grp[:2][::-1] + grp[2:]))
        self.index = {"grp": lax.axis_index("grp"), "in": lax.axis_index("in")}
        self.core = self.index["in"] & 1

    def swap(self, value, stage):
        pairs = []
        for g in range(self.groups):
            for i in range(self.inner):
                axis, bit = ("in", 0) if stage is None else self.orders[i & 1][stage]
                to = (g ^ (1 << bit), i) if axis == "grp" else (g, i ^ (1 << bit))
                pairs.append((g * self.inner + i, to[0] * self.inner + to[1]))
        return lax.ppermute(value, ("grp", "in"), pairs)

    def bit(self, stage):
        bits = [(self.index[axis] >> k) & 1 for axis, k in (order[stage] for order in self.orders)]
        return jnp.where(self.core == 0, bits[0], bits[1])

    def add_halves(self, kept, came):
        orders = self.orders

        def kernel(kept_ref, came_ref, sent_out, kept_out):
            bits = [(lax.axis_index(axis) >> k) & 1 for axis, k in (order[0] for order in orders)]
            bit = jnp.where(lax.axis_index("in") & 1 == 0, bits[0], bits[1])
            part = sent_out.shape[0]
            for out, place in ((sent_out, 1 - bit), (kept_out, bit)):
                rows = pl.ds(pl.multiple_of(place * part, part), part)
                out[...] = kept_ref[rows, :] + came_ref[rows, :]

        half = pltpu.VMEM((kept.shape[0] // 2, kept.shape[1]), F32)
        vmem = pl.BlockSpec(memory_space=pltpu.VMEM)
        return pl.pallas_call(
            kernel,
            in_specs=[vmem] * 2,
            out_specs=[vmem] * 2,
            out_shape=[half] * 2,
            compiler_params=pltpu.CompilerParams(vmem_limit_bytes=8 * 1024 * 1024),
            name="add_halves",
        )(kept, pltpu.with_memory_space_constraint(came, pltpu.VMEM))

    def all_sum(self, sent, kept):
        last = len(self.orders[0]) - 1
        came = self.swap(sent, None)
        if last:
            sent, kept = self.add_halves(kept, came)
            came = self.swap(sent, 0)
        for stage in range(1, last):
            bit = self.bit(stage)
            parts = [x.reshape(2, x.shape[0] // 2, x.shape[1]) for x in (kept, came)]

            def half(place):
                own, new = (lax.dynamic_index_in_dim(x, place, 0, keepdims=False) for x in parts)
                return own + new

            sent, kept = half(1 - bit), half(bit)
            came = self.swap(sent, stage)
        value = kept + came
        value = value + self.swap(value, last)
        for stage in range(last - 1, -1, -1):
            came = self.swap(value, stage)
            bit = self.bit(stage)
            whole = jnp.zeros((2,) + value.shape, value.dtype)
            whole = lax.dynamic_update_index_in_dim(whole, value, bit, 0)
            whole = lax.dynamic_update_index_in_dim(whole, came, 1 - bit, 0)
            value = whole.reshape(-1, value.shape[1])
        return value, self.swap(value, None)


def per_device(groups, inner, unfolding, start_basis):
    parts = gram(unfolding)
    halves = []
    for number in range(len(CHUNKS)):
        exchange = Exchange(groups, inner, number == 0)
        halves += exchange.all_sum(*parts[2 * number : 2 * number + 2])
    factor, core_block = iterate(start_basis, halves, unfolding)
    return (factor, core_block)


def solution(mesh):
    in_specs = (P(None, ("grp", "in")), P())
    out_specs = (P(), P(None, ("grp", "in")))
    body = functools.partial(per_device, mesh.shape["grp"], mesh.shape["in"])
    return jax.shard_map(body, mesh=mesh, in_specs=in_specs, out_specs=out_specs, check_vma=False)
```

```python
import functools

import jax
import jax.numpy as jnp
from jax import lax
from jax.experimental import pallas as pl
from jax.experimental.pallas import tpu as pltpu
from jax.sharding import PartitionSpec as P

ITERS = 3
BLOCKS = 4
F32 = jnp.float32
BF16 = jnp.bfloat16
NT = (((1,), (1,)), ((), ()))
NN = (((1,), (0,)), ((), ()))

CHUNKS = (
    ((0, 3), (1, 3), (2, 3), (3, 3), (0, 0)),
    ((0, 2), (1, 2), (2, 2), (0, 1), (1, 1)),
)


def split(value):
    high = value.astype(BF16)
    low = (value - high.astype(F32)).astype(BF16)
    return high, low


def split3(value):
    high = value.astype(BF16)
    return high, split(value - high.astype(F32))


def mm(left, right, dims):
    return lax.dot_general(left, right, dims, preferred_element_type=F32)


def units(chunk, bs):
    for i, j in chunk:
        yield i, j, 0, (bs // 2 if i == j else bs)
        yield i, j, 1, bs


def packed_rows(chunk, bs):
    return sum(rows for *_, rows in units(chunk, bs))


def pieces(chunk, bs):
    middle = packed_rows(chunk, bs) // 2
    base = 0
    for i, j, side, height in units(chunk, bs):
        cut = min(max(middle - base, 0), height)
        for lo, hi in ((0, cut), (cut, height)):
            if lo < hi:
                part = int(base + lo >= middle)
                first = base + lo - part * middle
                rows = slice(i * bs + lo, i * bs + hi)
                cols = slice(j * bs + side * (bs // 2), j * bs + (side + 1) * (bs // 2))
                yield part, slice(first, first + hi - lo), i == j and side, rows, cols
        base += height


def gram_kernel(bs, u_hbm, *refs):
    outs = refs[: 2 * len(CHUNKS)]
    u_ref, parts_ref, acc_ref, cross_ref, sems = refs[2 * len(CHUNKS) :]
    steps, _, width = u_ref.shape

    def copy(step, j):
        rows = slice(j * bs, (j + 1) * bs)
        cols = pl.ds(pl.multiple_of(step * width, width), width)
        return pltpu.make_async_copy(u_hbm.at[rows, cols], u_ref.at[step, rows, :], sems.at[step, j])

    for step in range(steps):
        for j in range(BLOCKS):
            copy(step, j).start()
    acc_ref[...] = jnp.zeros_like(acc_ref)
    cross_ref[...] = jnp.zeros_like(cross_ref)

    def body(step, carry):
        for j in range(BLOCKS):
            copy(step, j).wait()
            rows = slice(j * bs, (j + 1) * bs)
            high, low = split(u_ref[step, rows, :])
            for place, value in enumerate((high, high, low, high)):
                parts_ref[rows, place * width : (place + 1) * width] = value
        for j in range(BLOCKS):
            above, end = j * bs, (j + 1) * bs
            if j:
                acc_ref[:above, above:end] += mm(
                    parts_ref[:above, width : 4 * width], parts_ref[above:end, : 3 * width], NT
                )
            high = parts_ref[above:end, :width]
            acc_ref[above:end, above:end] += mm(high, high, NT)
            cross_ref[j] += mm(high, parts_ref[above:end, 2 * width : 3 * width], NT)
        return carry

    lax.fori_loop(0, steps, body, 0)
    core = lax.rem(lax.axis_index("in"), 2)
    for j in range(BLOCKS):
        above, end = j * bs, (j + 1) * bs
        acc_ref[above:end, above:end] += cross_ref[j] + cross_ref[j].T
    for mine in range(2):

        @pl.when(core == mine)
        def _():
            for number, chunk in enumerate(CHUNKS):
                sent, kept = outs[2 * number : 2 * number + 2]
                for part, place, _, rows, cols in pieces(chunk, bs):
                    (kept if part == mine else sent)[place, :] = acc_ref[rows, cols]


def gram(unfolding):
    order, depth = unfolding.shape
    bs = order // BLOCKS
    steps = 4
    width = depth // steps
    heights = [packed_rows(chunk, bs) for chunk in CHUNKS]
    halves = [(height // 2, bs // 2) for height in heights for _ in range(2)]
    return pl.pallas_call(
        functools.partial(gram_kernel, bs),
        in_specs=[pl.BlockSpec(memory_space=pl.ANY)],
        out_specs=[pl.BlockSpec(memory_space=pltpu.VMEM)] * len(halves),
        out_shape=[pltpu.VMEM(shape, F32) for shape in halves],
        scratch_shapes=[
            pltpu.VMEM((steps, order, width), F32),
            pltpu.VMEM((order, 4 * width), BF16),
            pltpu.VMEM((order, order), F32),
            pltpu.VMEM((BLOCKS, bs, bs), F32),
            pltpu.SemaphoreType.DMA((steps, BLOCKS)),
        ],
        compiler_params=pltpu.CompilerParams(vmem_limit_bytes=50 * 1024 * 1024),
        name="gram",
    )(unfolding)


def inverse_cholesky(inner):
    order = inner.shape[0]
    size = min(16, order)
    shape = (8, order)
    lane = lax.broadcasted_iota(jnp.int32, shape, 1)
    sub = lax.broadcasted_iota(jnp.int32, shape, 0)

    def lanes(value, k):
        return jnp.broadcast_to(value[:, k : k + 1], shape)

    def subs(value, i):
        return jnp.broadcast_to(value[i : i + 1, :], shape)

    def reciprocal(value):
        guess = pl.reciprocal(value, approx=True)
        return guess * (2.0 - value * guess)

    rows = [inner[m : m + 8, :] for m in range(0, order, 8)]
    result = []
    for first in range(0, order, size):
        inside = (lane >= first) & (lane < first + size)
        own = rows[first // 8 : (first + size) // 8]
        s = [[None] * (i + 1) for i in range(size)]
        for k in range(size):
            for g in range(k // 8, size // 8):
                column = lanes(own[g], first + k)
                for i in range(max(k, 8 * g), 8 * g + 8):
                    s[i][k] = subs(column, i - 8 * g)
        y = []
        for g in range(size // 8):
            unit = jnp.where(lane == first + 8 * g + sub, 1.0, 0.0)
            masked = jnp.where(inside, unit, own[g])
            y += [subs(masked, i) for i in range(8)]
        inverse = [None] * size
        f = [[None] * size for _ in range(size)]
        for k in range(size):
            inverse[k] = reciprocal(s[k][k])
            for i in range(k + 1, size):
                f[i][k] = s[i][k] * inverse[k]
            for i in range(k + 1, size):
                for j in range(k + 1, i + 1):
                    s[i][j] = s[i][j] - f[i][k] * s[j][k]
                y[i] = y[i] - f[i][k] * y[k]
        p = [y[k] * inverse[k] for k in range(size)]
        for j in range(size - 1, 0, -1):
            for i in range(j - 1, -1, -1):
                p[i] = p[i] - f[j][i] * p[j]
        for g in range(size // 8):
            out = y[8 * g] * lax.rsqrt(s[8 * g][8 * g])
            for i in range(1, 8):
                out = jnp.where(sub == i, y[8 * g + i] * lax.rsqrt(s[8 * g + i][8 * g + i]), out)
            result.append(jnp.where(lane <= first + 8 * g + sub, out, 0.0))
        for m in range((first + size) // 8, order // 8):
            value = jnp.where(inside, 0.0, rows[m])
            for k in range(size - 1, -1, -1):
                value = value - lanes(rows[m], first + k) * p[k]
            rows[m] = value
    return jnp.concatenate(result, axis=0)


def iterate_kernel(bs, start_hbm, *refs):
    count = 2 * len(CHUNKS)
    halves, refs = refs[:count], refs[count:]
    u_hbm, factor_hbm, core_hbm, *refs = refs
    g_high, g_low, both_ref, basis, parts_ref, u_vmem, factor_ref, core_ref, sems, out_sem = refs
    rank = basis.shape[0]
    half = bs // 2
    start_copy = pltpu.make_async_copy(start_hbm, factor_ref, sems.at[0])
    start_copy.start()
    copy = pltpu.make_async_copy(u_hbm, u_vmem, sems.at[1])
    copy.start()
    core = lax.rem(lax.axis_index("in"), 2)
    for mine in range(2):

        @pl.when(core == mine)
        def _():
            for number, chunk in enumerate(CHUNKS):
                own, other = halves[2 * number : 2 * number + 2]
                for part, place, lower, rows, cols in pieces(chunk, bs):
                    value = (own if part == mine else other)[place, :]
                    g_high[rows, cols], g_low[rows, cols] = split(value)
                    if lower and rows.start % bs == 0:
                        below = (slice(rows.start + half, rows.start + bs), slice(cols.start - half, cols.start))
                        g_high[below], g_low[below] = split(value[:half].T)

    start_copy.wait()
    high, low = split(factor_ref[...].T)
    both_ref[:rank, :] = high
    both_ref[rank:, :] = low

    def body(_, carry):
        for j in range(BLOCKS):
            above, end = j * bs, (j + 1) * bs
            total = mm(both_ref[:, :end], g_high[:end, above:end], NN)
            extra = mm(both_ref[:rank, :end], g_low[:end, above:end], NN)
            if j < BLOCKS - 1:
                total += mm(both_ref[:, end:], g_high[above:end, end:], NT)
                extra += mm(both_ref[:rank, end:], g_low[above:end, end:], NT)
            value = total[:rank] + (total[rank:] + extra)
            high, rest = split3(value)
            parts_ref[:rank, above:end] = rest[0]
            parts_ref[rank : 2 * rank, above:end] = high
            parts_ref[2 * rank :, above:end] = rest[1]
        product = mm(parts_ref[...], parts_ref[: 2 * rank, :], NT)
        cross = product[2 * rank :, rank:]
        inner = product[rank : 2 * rank, rank:] + (
            (product[:rank, rank:] + product[rank : 2 * rank, :rank])
            + (product[:rank, :rank] + (cross + cross.T))
        )
        high, (middle, low) = split3(inverse_cholesky(inner))
        left = jnp.concatenate(
            [
                jnp.concatenate([middle, high], axis=1),
                jnp.concatenate([high, middle], axis=1),
            ],
            axis=0,
        )
        last = jnp.concatenate([low, high], axis=1)
        for j in range(BLOCKS):
            cols = slice(j * bs, (j + 1) * bs)
            product = mm(left, parts_ref[: 2 * rank, cols], NN)
            product = product[:rank] + (product[rank:] + mm(last, parts_ref[rank:, cols], NN))
            basis[:, cols] = product
            both_ref[:rank, cols], both_ref[rank:, cols] = split(product)
        return carry

    lax.fori_loop(0, ITERS, body, 0)
    factor_ref[...] = basis[...].T
    depth = u_vmem.shape[1]
    step = min(512, depth)
    outs = [pltpu.make_async_copy(factor_ref, factor_hbm, out_sem.at[0])]
    outs[0].start()
    copy.wait()
    for number, lo in enumerate(range(0, depth, step)):
        cols = slice(lo, lo + step)
        u_high, u_low = split(u_vmem[:, cols])
        total = mm(both_ref[...], u_high, NN)
        core_ref[:, cols] = total[:rank] + (total[rank:] + mm(both_ref[:rank, :], u_low, NN))
        outs.append(
            pltpu.make_async_copy(core_ref.at[:, cols], core_hbm.at[:, cols], out_sem.at[number + 1])
        )
        outs[-1].start()
    for out in outs:
        out.wait()


def iterate(start, halves, unfolding):
    order, rank = start.shape
    depth = unfolding.shape[1]
    bs = order // BLOCKS
    vmem = pl.BlockSpec(memory_space=pltpu.VMEM)
    hbm = pl.BlockSpec(memory_space=pl.ANY)
    return pl.pallas_call(
        functools.partial(iterate_kernel, bs),
        in_specs=[hbm] + [vmem] * len(halves) + [hbm],
        out_specs=[hbm, hbm],
        out_shape=[
            jax.ShapeDtypeStruct((order, rank), F32),
            jax.ShapeDtypeStruct((rank, depth), F32),
        ],
        scratch_shapes=[
            pltpu.VMEM((order, order), BF16),
            pltpu.VMEM((order, order), BF16),
            pltpu.VMEM((2 * rank, order), BF16),
            pltpu.VMEM((rank, order), F32),
            pltpu.VMEM((3 * rank, order), BF16),
            pltpu.VMEM((order, depth), F32),
            pltpu.VMEM((order, rank), F32),
            pltpu.VMEM((rank, depth), F32),
            pltpu.SemaphoreType.DMA((2,)),
            pltpu.SemaphoreType.DMA((1 + depth // min(512, depth),)),
        ],
        compiler_params=pltpu.CompilerParams(vmem_limit_bytes=36 * 1024 * 1024),
        name="iterate",
    )(start, *halves, unfolding)


class Exchange:
    def __init__(self, groups, inner, inner_first):
        self.groups, self.inner = groups, inner
        grp = [("grp", k) for k in range(groups.bit_length() - 1)]
        rest = [("in", k) for k in range(1, inner.bit_length() - 1)]
        before, after = (rest[:1], rest[1:]) if inner_first else ([], rest)
        self.orders = tuple(before + g + after for g in (grp, grp[:2][::-1] + grp[2:]))
        self.index = {"grp": lax.axis_index("grp"), "in": lax.axis_index("in")}
        self.core = self.index["in"] & 1

    def swap(self, value, stage):
        pairs = []
        for g in range(self.groups):
            for i in range(self.inner):
                axis, bit = ("in", 0) if stage is None else self.orders[i & 1][stage]
                to = (g ^ (1 << bit), i) if axis == "grp" else (g, i ^ (1 << bit))
                pairs.append((g * self.inner + i, to[0] * self.inner + to[1]))
        return lax.ppermute(value, ("grp", "in"), pairs)

    def bit(self, stage):
        bits = [(self.index[axis] >> k) & 1 for axis, k in (order[stage] for order in self.orders)]
        return jnp.where(self.core == 0, bits[0], bits[1])

    def add_halves(self, kept, came):
        orders = self.orders

        def kernel(kept_ref, came_ref, sent_out, kept_out):
            bits = [(lax.axis_index(axis) >> k) & 1 for axis, k in (order[0] for order in orders)]
            bit = jnp.where(lax.axis_index("in") & 1 == 0, bits[0], bits[1])
            part = sent_out.shape[0]
            for out, place in ((sent_out, 1 - bit), (kept_out, bit)):
                rows = pl.ds(pl.multiple_of(place * part, part), part)
                out[...] = kept_ref[rows, :] + came_ref[rows, :]

        half = pltpu.VMEM((kept.shape[0] // 2, kept.shape[1]), F32)
        vmem = pl.BlockSpec(memory_space=pltpu.VMEM)
        return pl.pallas_call(
            kernel,
            in_specs=[vmem] * 2,
            out_specs=[vmem] * 2,
            out_shape=[half] * 2,
            compiler_params=pltpu.CompilerParams(vmem_limit_bytes=8 * 1024 * 1024),
            name="add_halves",
        )(kept, pltpu.with_memory_space_constraint(came, pltpu.VMEM))

    def all_sum(self, sent, kept):
        last = len(self.orders[0]) - 1
        came = self.swap(sent, None)
        if last:
            sent, kept = self.add_halves(kept, came)
            came = self.swap(sent, 0)
        for stage in range(1, last):
            bit = self.bit(stage)
            parts = [x.reshape(2, x.shape[0] // 2, x.shape[1]) for x in (kept, came)]

            def half(place):
                own, new = (lax.dynamic_index_in_dim(x, place, 0, keepdims=False) for x in parts)
                return own + new

            sent, kept = half(1 - bit), half(bit)
            came = self.swap(sent, stage)
        value = kept + came
        value = value + self.swap(value, last)
        for stage in range(last - 1, -1, -1):
            came = self.swap(value, stage)
            bit = self.bit(stage)
            whole = jnp.zeros((2,) + value.shape, value.dtype)
            whole = lax.dynamic_update_index_in_dim(whole, value, bit, 0)
            whole = lax.dynamic_update_index_in_dim(whole, came, 1 - bit, 0)
            value = whole.reshape(-1, value.shape[1])
        return value, self.swap(value, None)


def per_device(groups, inner, unfolding, start_basis):
    parts = gram(unfolding)
    halves = []
    for number in range(len(CHUNKS)):
        exchange = Exchange(groups, inner, number == 0)
        halves += exchange.all_sum(*parts[2 * number : 2 * number + 2])
    factor, core_block = iterate(start_basis, halves, unfolding)
    return (factor, core_block)


def solution(mesh):
    in_specs = (P(None, ("grp", "in")), P())
    out_specs = (P(), P(None, ("grp", "in")))
    body = functools.partial(per_device, mesh.shape["grp"], mesh.shape["in"])
    return jax.shard_map(body, mesh=mesh, in_specs=in_specs, out_specs=out_specs, check_vma=False)
```

```python
import functools

import jax
import jax.numpy as jnp
from jax import lax
from jax.experimental import pallas as pl
from jax.experimental.pallas import tpu as pltpu
from jax.sharding import PartitionSpec as P

ITERS = 3
BLOCKS = 4
F32 = jnp.float32
BF16 = jnp.bfloat16
NT = (((1,), (1,)), ((), ()))
NN = (((1,), (0,)), ((), ()))

CHUNKS = (
    ((0, 3), (1, 3), (2, 3), (3, 3), (0, 0)),
    ((0, 2), (1, 2), (2, 2), (0, 1), (1, 1)),
)


def split(value):
    high = value.astype(BF16)
    low = (value - high.astype(F32)).astype(BF16)
    return high, low


def split3(value):
    high = value.astype(BF16)
    return high, split(value - high.astype(F32))


def mm(left, right, dims):
    return lax.dot_general(left, right, dims, preferred_element_type=F32)


def units(chunk, bs):
    for i, j in chunk:
        yield i, j, 0, (bs // 2 if i == j else bs)
        yield i, j, 1, bs


def packed_rows(chunk, bs):
    return sum(rows for *_, rows in units(chunk, bs))


def pieces(chunk, bs):
    middle = packed_rows(chunk, bs) // 2
    base = 0
    for i, j, side, height in units(chunk, bs):
        cut = min(max(middle - base, 0), height)
        for lo, hi in ((0, cut), (cut, height)):
            if lo < hi:
                part = int(base + lo >= middle)
                first = base + lo - part * middle
                rows = slice(i * bs + lo, i * bs + hi)
                cols = slice(j * bs + side * (bs // 2), j * bs + (side + 1) * (bs // 2))
                yield part, slice(first, first + hi - lo), i == j and side, rows, cols
        base += height


def gram_kernel(bs, u_hbm, *refs):
    outs = refs[: 2 * len(CHUNKS)]
    u_ref, parts_ref, acc_ref, cross_ref, sems = refs[2 * len(CHUNKS) :]
    steps, _, width = u_ref.shape

    def copy(step):
        cols = pl.ds(pl.multiple_of(step * width, width), width)
        return pltpu.make_async_copy(u_hbm.at[:, cols], u_ref.at[step], sems.at[step])

    for step in range(steps):
        copy(step).start()
    acc_ref[...] = jnp.zeros_like(acc_ref)
    cross_ref[...] = jnp.zeros_like(cross_ref)

    def body(step, carry):
        copy(step).wait()
        for j in range(BLOCKS):
            rows = slice(j * bs, (j + 1) * bs)
            high, low = split(u_ref[step, rows, :])
            for place, value in enumerate((high, high, low, high)):
                parts_ref[rows, place * width : (place + 1) * width] = value
        for j in range(BLOCKS):
            above, end = j * bs, (j + 1) * bs
            if j:
                acc_ref[:above, above:end] += mm(
                    parts_ref[:above, width : 4 * width], parts_ref[above:end, : 3 * width], NT
                )
            high = parts_ref[above:end, :width]
            acc_ref[above:end, above:end] += mm(high, high, NT)
            cross_ref[j] += mm(high, parts_ref[above:end, 2 * width : 3 * width], NT)
        return carry

    lax.fori_loop(0, steps, body, 0)
    core = lax.rem(lax.axis_index("in"), 2)
    for j in range(BLOCKS):
        above, end = j * bs, (j + 1) * bs
        acc_ref[above:end, above:end] += cross_ref[j] + cross_ref[j].T
    for mine in range(2):

        @pl.when(core == mine)
        def _():
            for number, chunk in enumerate(CHUNKS):
                sent, kept = outs[2 * number : 2 * number + 2]
                for part, place, _, rows, cols in pieces(chunk, bs):
                    (kept if part == mine else sent)[place, :] = acc_ref[rows, cols]


def gram(unfolding):
    order, depth = unfolding.shape
    bs = order // BLOCKS
    steps = 4
    width = depth // steps
    heights = [packed_rows(chunk, bs) for chunk in CHUNKS]
    halves = [(height // 2, bs // 2) for height in heights for _ in range(2)]
    return pl.pallas_call(
        functools.partial(gram_kernel, bs),
        in_specs=[pl.BlockSpec(memory_space=pl.ANY)],
        out_specs=[pl.BlockSpec(memory_space=pltpu.VMEM)] * len(halves),
        out_shape=[pltpu.VMEM(shape, F32) for shape in halves],
        scratch_shapes=[
            pltpu.VMEM((steps, order, width), F32),
            pltpu.VMEM((order, 4 * width), BF16),
            pltpu.VMEM((order, order), F32),
            pltpu.VMEM((BLOCKS, bs, bs), F32),
            pltpu.SemaphoreType.DMA((steps,)),
        ],
        compiler_params=pltpu.CompilerParams(vmem_limit_bytes=50 * 1024 * 1024),
        name="gram",
    )(unfolding)


def inverse_cholesky(inner):
    order = inner.shape[0]
    size = min(16, order)
    shape = (8, order)
    lane = lax.broadcasted_iota(jnp.int32, shape, 1)
    sub = lax.broadcasted_iota(jnp.int32, shape, 0)

    def lanes(value, k):
        return jnp.broadcast_to(value[:, k : k + 1], shape)

    def subs(value, i):
        return jnp.broadcast_to(value[i : i + 1, :], shape)

    def reciprocal(value):
        guess = pl.reciprocal(value, approx=True)
        return guess * (2.0 - value * guess)

    rows = [inner[m : m + 8, :] for m in range(0, order, 8)]
    result = []
    for first in range(0, order, size):
        inside = (lane >= first) & (lane < first + size)
        own = rows[first // 8 : (first + size) // 8]
        s = [[None] * (i + 1) for i in range(size)]
        for k in range(size):
            for g in range(k // 8, size // 8):
                column = lanes(own[g], first + k)
                for i in range(max(k, 8 * g), 8 * g + 8):
                    s[i][k] = subs(column, i - 8 * g)
        y = []
        for g in range(size // 8):
            unit = jnp.where(lane == first + 8 * g + sub, 1.0, 0.0)
            masked = jnp.where(inside, unit, own[g])
            y += [subs(masked, i) for i in range(8)]
        inverse = [None] * size
        f = [[None] * size for _ in range(size)]
        for k in range(size):
            inverse[k] = reciprocal(s[k][k])
            for i in range(k + 1, size):
                f[i][k] = s[i][k] * inverse[k]
            for i in range(k + 1, size):
                for j in range(k + 1, i + 1):
                    s[i][j] = s[i][j] - f[i][k] * s[j][k]
                y[i] = y[i] - f[i][k] * y[k]
        p = [y[k] * inverse[k] for k in range(size)]
        for j in range(size - 1, 0, -1):
            for i in range(j - 1, -1, -1):
                p[i] = p[i] - f[j][i] * p[j]
        for g in range(size // 8):
            out = y[8 * g] * lax.rsqrt(s[8 * g][8 * g])
            for i in range(1, 8):
                out = jnp.where(sub == i, y[8 * g + i] * lax.rsqrt(s[8 * g + i][8 * g + i]), out)
            result.append(jnp.where(lane <= first + 8 * g + sub, out, 0.0))
        for m in range((first + size) // 8, order // 8):
            value = jnp.where(inside, 0.0, rows[m])
            for k in range(size - 1, -1, -1):
                value = value - lanes(rows[m], first + k) * p[k]
            rows[m] = value
    return jnp.concatenate(result, axis=0)


def iterate_kernel(bs, start_hbm, *refs):
    count = 2 * len(CHUNKS)
    halves, refs = refs[:count], refs[count:]
    u_hbm, factor_hbm, core_hbm, *refs = refs
    g_high, g_low, both_ref, basis, parts_ref, u_vmem, factor_ref, core_ref, sems, out_sem = refs
    rank = basis.shape[0]
    half = bs // 2
    start_copy = pltpu.make_async_copy(start_hbm, factor_ref, sems.at[0])
    start_copy.start()
    copy = pltpu.make_async_copy(u_hbm, u_vmem, sems.at[1])
    copy.start()
    core = lax.rem(lax.axis_index("in"), 2)
    for mine in range(2):

        @pl.when(core == mine)
        def _():
            for number, chunk in enumerate(CHUNKS):
                own, other = halves[2 * number : 2 * number + 2]
                for part, place, lower, rows, cols in pieces(chunk, bs):
                    value = (own if part == mine else other)[place, :]
                    g_high[rows, cols], g_low[rows, cols] = split(value)
                    if lower and rows.start % bs == 0:
                        below = (slice(rows.start + half, rows.start + bs), slice(cols.start - half, cols.start))
                        g_high[below], g_low[below] = split(value[:half].T)

    start_copy.wait()
    high, low = split(factor_ref[...].T)
    both_ref[:rank, :] = high
    both_ref[rank:, :] = low

    def body(_, carry):
        for j in range(BLOCKS):
            above, end = j * bs, (j + 1) * bs
            total = mm(both_ref[:, :end], g_high[:end, above:end], NN)
            extra = mm(both_ref[:rank, :end], g_low[:end, above:end], NN)
            if j < BLOCKS - 1:
                total += mm(both_ref[:, end:], g_high[above:end, end:], NT)
                extra += mm(both_ref[:rank, end:], g_low[above:end, end:], NT)
            value = total[:rank] + (total[rank:] + extra)
            high, rest = split3(value)
            parts_ref[:rank, above:end] = rest[0]
            parts_ref[rank : 2 * rank, above:end] = high
            parts_ref[2 * rank :, above:end] = rest[1]
        product = mm(parts_ref[...], parts_ref[: 2 * rank, :], NT)
        cross = product[2 * rank :, rank:]
        inner = product[rank : 2 * rank, rank:] + (
            (product[:rank, rank:] + product[rank : 2 * rank, :rank])
            + (product[:rank, :rank] + (cross + cross.T))
        )
        high, (middle, low) = split3(inverse_cholesky(inner))
        left = jnp.concatenate(
            [
                jnp.concatenate([middle, high], axis=1),
                jnp.concatenate([high, middle], axis=1),
            ],
            axis=0,
        )
        last = jnp.concatenate([low, high], axis=1)
        for j in range(BLOCKS):
            cols = slice(j * bs, (j + 1) * bs)
            product = mm(left, parts_ref[: 2 * rank, cols], NN)
            product = product[:rank] + (product[rank:] + mm(last, parts_ref[rank:, cols], NN))
            basis[:, cols] = product
            both_ref[:rank, cols], both_ref[rank:, cols] = split(product)
        return carry

    lax.fori_loop(0, ITERS, body, 0)
    factor_ref[...] = basis[...].T
    depth = u_vmem.shape[1]
    step = min(512, depth)
    outs = [pltpu.make_async_copy(factor_ref, factor_hbm, out_sem.at[0])]
    outs[0].start()
    copy.wait()
    for number, lo in enumerate(range(0, depth, step)):
        cols = slice(lo, lo + step)
        u_high, u_low = split(u_vmem[:, cols])
        total = mm(both_ref[...], u_high, NN)
        core_ref[:, cols] = total[:rank] + (total[rank:] + mm(both_ref[:rank, :], u_low, NN))
        outs.append(
            pltpu.make_async_copy(core_ref.at[:, cols], core_hbm.at[:, cols], out_sem.at[number + 1])
        )
        outs[-1].start()
    for out in outs:
        out.wait()


def iterate(start, halves, unfolding):
    order, rank = start.shape
    depth = unfolding.shape[1]
    bs = order // BLOCKS
    vmem = pl.BlockSpec(memory_space=pltpu.VMEM)
    hbm = pl.BlockSpec(memory_space=pl.ANY)
    return pl.pallas_call(
        functools.partial(iterate_kernel, bs),
        in_specs=[hbm] + [vmem] * len(halves) + [hbm],
        out_specs=[hbm, hbm],
        out_shape=[
            jax.ShapeDtypeStruct((order, rank), F32),
            jax.ShapeDtypeStruct((rank, depth), F32),
        ],
        scratch_shapes=[
            pltpu.VMEM((order, order), BF16),
            pltpu.VMEM((order, order), BF16),
            pltpu.VMEM((2 * rank, order), BF16),
            pltpu.VMEM((rank, order), F32),
            pltpu.VMEM((3 * rank, order), BF16),
            pltpu.VMEM((order, depth), F32),
            pltpu.VMEM((order, rank), F32),
            pltpu.VMEM((rank, depth), F32),
            pltpu.SemaphoreType.DMA((2,)),
            pltpu.SemaphoreType.DMA((1 + depth // min(512, depth),)),
        ],
        compiler_params=pltpu.CompilerParams(vmem_limit_bytes=36 * 1024 * 1024),
        name="iterate",
    )(start, *halves, unfolding)


class Exchange:
    def __init__(self, groups, inner, inner_first):
        self.groups, self.inner = groups, inner
        grp = [("grp", k) for k in range(groups.bit_length() - 1)]
        rest = [("in", k) for k in range(1, inner.bit_length() - 1)]
        before, after = (rest[:1], rest[1:]) if inner_first else ([], rest)
        self.orders = tuple(before + g + after for g in (grp, grp[:2][::-1] + grp[2:]))
        self.index = {"grp": lax.axis_index("grp"), "in": lax.axis_index("in")}
        self.core = self.index["in"] & 1

    def swap(self, value, stage):
        pairs = []
        for g in range(self.groups):
            for i in range(self.inner):
                axis, bit = ("in", 0) if stage is None else self.orders[i & 1][stage]
                to = (g ^ (1 << bit), i) if axis == "grp" else (g, i ^ (1 << bit))
                pairs.append((g * self.inner + i, to[0] * self.inner + to[1]))
        return lax.ppermute(value, ("grp", "in"), pairs)

    def bit(self, stage):
        bits = [(self.index[axis] >> k) & 1 for axis, k in (order[stage] for order in self.orders)]
        return jnp.where(self.core == 0, bits[0], bits[1])

    def add_halves(self, kept, came):
        orders = self.orders

        def kernel(kept_ref, came_ref, sent_out, kept_out):
            bits = [(lax.axis_index(axis) >> k) & 1 for axis, k in (order[0] for order in orders)]
            bit = jnp.where(lax.axis_index("in") & 1 == 0, bits[0], bits[1])
            part = sent_out.shape[0]
            for out, place in ((sent_out, 1 - bit), (kept_out, bit)):
                rows = pl.ds(pl.multiple_of(place * part, part), part)
                out[...] = kept_ref[rows, :] + came_ref[rows, :]

        half = pltpu.VMEM((kept.shape[0] // 2, kept.shape[1]), F32)
        vmem = pl.BlockSpec(memory_space=pltpu.VMEM)
        return pl.pallas_call(
            kernel,
            in_specs=[vmem] * 2,
            out_specs=[vmem] * 2,
            out_shape=[half] * 2,
            compiler_params=pltpu.CompilerParams(vmem_limit_bytes=8 * 1024 * 1024),
            name="add_halves",
        )(kept, pltpu.with_memory_space_constraint(came, pltpu.VMEM))

    def all_sum(self, sent, kept):
        last = len(self.orders[0]) - 1
        came = self.swap(sent, None)
        if last:
            sent, kept = self.add_halves(kept, came)
            came = self.swap(sent, 0)
        for stage in range(1, last):
            bit = self.bit(stage)
            parts = [x.reshape(2, x.shape[0] // 2, x.shape[1]) for x in (kept, came)]

            def half(place):
                own, new = (lax.dynamic_index_in_dim(x, place, 0, keepdims=False) for x in parts)
                return own + new

            sent, kept = half(1 - bit), half(bit)
            came = self.swap(sent, stage)
        value = kept + came
        value = value + self.swap(value, last)
        for stage in range(last - 1, -1, -1):
            came = self.swap(value, stage)
            bit = self.bit(stage)
            whole = jnp.zeros((2,) + value.shape, value.dtype)
            whole = lax.dynamic_update_index_in_dim(whole, value, bit, 0)
            whole = lax.dynamic_update_index_in_dim(whole, came, 1 - bit, 0)
            value = whole.reshape(-1, value.shape[1])
        return value, self.swap(value, None)


def per_device(groups, inner, unfolding, start_basis):
    parts = gram(unfolding)
    halves = []
    for number in range(len(CHUNKS)):
        exchange = Exchange(groups, inner, number == 0)
        halves += exchange.all_sum(*parts[2 * number : 2 * number + 2])
    factor, core_block = iterate(start_basis, halves, unfolding)
    return (factor, core_block)


def solution(mesh):
    in_specs = (P(None, ("grp", "in")), P())
    out_specs = (P(), P(None, ("grp", "in")))
    body = functools.partial(per_device, mesh.shape["grp"], mesh.shape["in"])
    return jax.shard_map(body, mesh=mesh, in_specs=in_specs, out_specs=out_specs, check_vma=False)
```

```python
import functools

import jax
import jax.numpy as jnp
from jax import lax
from jax.experimental import pallas as pl
from jax.experimental.pallas import tpu as pltpu
from jax.sharding import PartitionSpec as P

ITERS = 3
BLOCKS = 4
F32 = jnp.float32
BF16 = jnp.bfloat16
NT = (((1,), (1,)), ((), ()))
NN = (((1,), (0,)), ((), ()))

CHUNKS = (
    ((0, 3), (1, 3), (2, 3), (3, 3), (0, 0)),
    ((0, 2), (1, 2), (2, 2), (0, 1), (1, 1)),
)


def split(value):
    high = value.astype(BF16)
    low = (value - high.astype(F32)).astype(BF16)
    return high, low


def split3(value):
    high = value.astype(BF16)
    return high, split(value - high.astype(F32))


def mm(left, right, dims):
    return lax.dot_general(left, right, dims, preferred_element_type=F32)


def units(chunk, bs):
    for i, j in chunk:
        yield i, j, 0, (bs // 2 if i == j else bs)
        yield i, j, 1, bs


def packed_rows(chunk, bs):
    return sum(rows for *_, rows in units(chunk, bs))


def pieces(chunk, bs):
    middle = packed_rows(chunk, bs) // 2
    base = 0
    for i, j, side, height in units(chunk, bs):
        cut = min(max(middle - base, 0), height)
        for lo, hi in ((0, cut), (cut, height)):
            if lo < hi:
                part = int(base + lo >= middle)
                first = base + lo - part * middle
                rows = slice(i * bs + lo, i * bs + hi)
                cols = slice(j * bs + side * (bs // 2), j * bs + (side + 1) * (bs // 2))
                yield part, slice(first, first + hi - lo), i == j and side, rows, cols
        base += height


def gram_kernel(bs, u_hbm, *refs):
    outs = refs[: 2 * len(CHUNKS)]
    u_ref, parts_ref, acc_ref, cross_ref, sems = refs[2 * len(CHUNKS) :]
    steps, _, width = u_ref.shape

    def copy(step):
        cols = pl.ds(pl.multiple_of(step * width, width), width)
        return pltpu.make_async_copy(u_hbm.at[:, cols], u_ref.at[step], sems.at[step])

    for step in range(steps):
        copy(step).start()
    acc_ref[...] = jnp.zeros_like(acc_ref)
    cross_ref[...] = jnp.zeros_like(cross_ref)

    def body(step, carry):
        copy(step).wait()
        for j in range(BLOCKS):
            rows = slice(j * bs, (j + 1) * bs)
            high, low = split(u_ref[step, rows, :])
            for place, value in enumerate((high, high, low, high)):
                parts_ref[rows, place * width : (place + 1) * width] = value
            above, end = j * bs, (j + 1) * bs
            if j:
                acc_ref[:above, above:end] += mm(
                    parts_ref[:above, width : 4 * width], parts_ref[above:end, : 3 * width], NT
                )
            high = parts_ref[above:end, :width]
            acc_ref[above:end, above:end] += mm(high, high, NT)
            cross_ref[j] += mm(high, parts_ref[above:end, 2 * width : 3 * width], NT)
        return carry

    lax.fori_loop(0, steps, body, 0)
    core = lax.rem(lax.axis_index("in"), 2)
    for j in range(BLOCKS):
        above, end = j * bs, (j + 1) * bs
        acc_ref[above:end, above:end] += cross_ref[j] + cross_ref[j].T
    for mine in range(2):

        @pl.when(core == mine)
        def _():
            for number, chunk in enumerate(CHUNKS):
                sent, kept = outs[2 * number : 2 * number + 2]
                for part, place, _, rows, cols in pieces(chunk, bs):
                    (kept if part == mine else sent)[place, :] = acc_ref[rows, cols]


def gram(unfolding):
    order, depth = unfolding.shape
    bs = order // BLOCKS
    steps = 4
    width = depth // steps
    heights = [packed_rows(chunk, bs) for chunk in CHUNKS]
    halves = [(height // 2, bs // 2) for height in heights for _ in range(2)]
    return pl.pallas_call(
        functools.partial(gram_kernel, bs),
        in_specs=[pl.BlockSpec(memory_space=pl.ANY)],
        out_specs=[pl.BlockSpec(memory_space=pltpu.VMEM)] * len(halves),
        out_shape=[pltpu.VMEM(shape, F32) for shape in halves],
        scratch_shapes=[
            pltpu.VMEM((steps, order, width), F32),
            pltpu.VMEM((order, 4 * width), BF16),
            pltpu.VMEM((order, order), F32),
            pltpu.VMEM((BLOCKS, bs, bs), F32),
            pltpu.SemaphoreType.DMA((steps,)),
        ],
        compiler_params=pltpu.CompilerParams(vmem_limit_bytes=50 * 1024 * 1024),
        name="gram",
    )(unfolding)


def inverse_cholesky(inner):
    order = inner.shape[0]
    size = min(16, order)
    shape = (8, order)
    lane = lax.broadcasted_iota(jnp.int32, shape, 1)
    sub = lax.broadcasted_iota(jnp.int32, shape, 0)

    def lanes(value, k):
        return jnp.broadcast_to(value[:, k : k + 1], shape)

    def subs(value, i):
        return jnp.broadcast_to(value[i : i + 1, :], shape)

    def reciprocal(value):
        guess = pl.reciprocal(value, approx=True)
        return guess * (2.0 - value * guess)

    rows = [inner[m : m + 8, :] for m in range(0, order, 8)]
    result = []
    for first in range(0, order, size):
        inside = (lane >= first) & (lane < first + size)
        own = rows[first // 8 : (first + size) // 8]
        s = [[None] * (i + 1) for i in range(size)]
        for k in range(size):
            for g in range(k // 8, size // 8):
                column = lanes(own[g], first + k)
                for i in range(max(k, 8 * g), 8 * g + 8):
                    s[i][k] = subs(column, i - 8 * g)
        y = []
        for g in range(size // 8):
            unit = jnp.where(lane == first + 8 * g + sub, 1.0, 0.0)
            masked = jnp.where(inside, unit, own[g])
            y += [subs(masked, i) for i in range(8)]
        inverse = [None] * size
        f = [[None] * size for _ in range(size)]
        for k in range(size):
            inverse[k] = reciprocal(s[k][k])
            for i in range(k + 1, size):
                f[i][k] = s[i][k] * inverse[k]
            for i in range(k + 1, size):
                for j in range(k + 1, i + 1):
                    s[i][j] = s[i][j] - f[i][k] * s[j][k]
                y[i] = y[i] - f[i][k] * y[k]
        p = [y[k] * inverse[k] for k in range(size)]
        for j in range(size - 1, 0, -1):
            for i in range(j - 1, -1, -1):
                p[i] = p[i] - f[j][i] * p[j]
        for g in range(size // 8):
            out = y[8 * g] * lax.rsqrt(s[8 * g][8 * g])
            for i in range(1, 8):
                out = jnp.where(sub == i, y[8 * g + i] * lax.rsqrt(s[8 * g + i][8 * g + i]), out)
            result.append(jnp.where(lane <= first + 8 * g + sub, out, 0.0))
        for m in range((first + size) // 8, order // 8):
            value = jnp.where(inside, 0.0, rows[m])
            for k in range(size - 1, -1, -1):
                value = value - lanes(rows[m], first + k) * p[k]
            rows[m] = value
    return jnp.concatenate(result, axis=0)


def iterate_kernel(bs, start_hbm, *refs):
    count = 2 * len(CHUNKS)
    halves, refs = refs[:count], refs[count:]
    u_hbm, factor_hbm, core_hbm, *refs = refs
    g_high, g_low, both_ref, basis, parts_ref, u_vmem, factor_ref, core_ref, sems, out_sem = refs
    rank = basis.shape[0]
    half = bs // 2
    start_copy = pltpu.make_async_copy(start_hbm, factor_ref, sems.at[0])
    start_copy.start()
    copy = pltpu.make_async_copy(u_hbm, u_vmem, sems.at[1])
    copy.start()
    core = lax.rem(lax.axis_index("in"), 2)
    for mine in range(2):

        @pl.when(core == mine)
        def _():
            for number, chunk in enumerate(CHUNKS):
                own, other = halves[2 * number : 2 * number + 2]
                for part, place, lower, rows, cols in pieces(chunk, bs):
                    value = (own if part == mine else other)[place, :]
                    g_high[rows, cols], g_low[rows, cols] = split(value)
                    if lower and rows.start % bs == 0:
                        below = (slice(rows.start + half, rows.start + bs), slice(cols.start - half, cols.start))
                        g_high[below], g_low[below] = split(value[:half].T)

    start_copy.wait()
    high, low = split(factor_ref[...].T)
    both_ref[:rank, :] = high
    both_ref[rank:, :] = low

    def body(_, carry):
        for j in range(BLOCKS):
            above, end = j * bs, (j + 1) * bs
            total = mm(both_ref[:, :end], g_high[:end, above:end], NN)
            extra = mm(both_ref[:rank, :end], g_low[:end, above:end], NN)
            if j < BLOCKS - 1:
                total += mm(both_ref[:, end:], g_high[above:end, end:], NT)
                extra += mm(both_ref[:rank, end:], g_low[above:end, end:], NT)
            value = total[:rank] + (total[rank:] + extra)
            high, rest = split3(value)
            parts_ref[:rank, above:end] = rest[0]
            parts_ref[rank : 2 * rank, above:end] = high
            parts_ref[2 * rank :, above:end] = rest[1]
        product = mm(parts_ref[...], parts_ref[: 2 * rank, :], NT)
        cross = product[2 * rank :, rank:]
        inner = product[rank : 2 * rank, rank:] + (
            (product[:rank, rank:] + product[rank : 2 * rank, :rank])
            + (product[:rank, :rank] + (cross + cross.T))
        )
        high, (middle, low) = split3(inverse_cholesky(inner))
        left = jnp.concatenate(
            [
                jnp.concatenate([middle, high], axis=1),
                jnp.concatenate([high, middle], axis=1),
            ],
            axis=0,
        )
        last = jnp.concatenate([low, high], axis=1)
        for j in range(BLOCKS):
            cols = slice(j * bs, (j + 1) * bs)
            product = mm(left, parts_ref[: 2 * rank, cols], NN)
            product = product[:rank] + (product[rank:] + mm(last, parts_ref[rank:, cols], NN))
            basis[:, cols] = product
            both_ref[:rank, cols], both_ref[rank:, cols] = split(product)
        return carry

    lax.fori_loop(0, ITERS, body, 0)
    factor_ref[...] = basis[...].T
    depth = u_vmem.shape[1]
    step = min(512, depth)
    outs = [pltpu.make_async_copy(factor_ref, factor_hbm, out_sem.at[0])]
    outs[0].start()
    copy.wait()
    for number, lo in enumerate(range(0, depth, step)):
        cols = slice(lo, lo + step)
        u_high, u_low = split(u_vmem[:, cols])
        total = mm(both_ref[...], u_high, NN)
        core_ref[:, cols] = total[:rank] + (total[rank:] + mm(both_ref[:rank, :], u_low, NN))
        outs.append(
            pltpu.make_async_copy(core_ref.at[:, cols], core_hbm.at[:, cols], out_sem.at[number + 1])
        )
        outs[-1].start()
    for out in outs:
        out.wait()


def iterate(start, halves, unfolding):
    order, rank = start.shape
    depth = unfolding.shape[1]
    bs = order // BLOCKS
    vmem = pl.BlockSpec(memory_space=pltpu.VMEM)
    hbm = pl.BlockSpec(memory_space=pl.ANY)
    return pl.pallas_call(
        functools.partial(iterate_kernel, bs),
        in_specs=[hbm] + [vmem] * len(halves) + [hbm],
        out_specs=[hbm, hbm],
        out_shape=[
            jax.ShapeDtypeStruct((order, rank), F32),
            jax.ShapeDtypeStruct((rank, depth), F32),
        ],
        scratch_shapes=[
            pltpu.VMEM((order, order), BF16),
            pltpu.VMEM((order, order), BF16),
            pltpu.VMEM((2 * rank, order), BF16),
            pltpu.VMEM((rank, order), F32),
            pltpu.VMEM((3 * rank, order), BF16),
            pltpu.VMEM((order, depth), F32),
            pltpu.VMEM((order, rank), F32),
            pltpu.VMEM((rank, depth), F32),
            pltpu.SemaphoreType.DMA((2,)),
            pltpu.SemaphoreType.DMA((1 + depth // min(512, depth),)),
        ],
        compiler_params=pltpu.CompilerParams(vmem_limit_bytes=36 * 1024 * 1024),
        name="iterate",
    )(start, *halves, unfolding)


class Exchange:
    def __init__(self, groups, inner, inner_first):
        self.groups, self.inner = groups, inner
        grp = [("grp", k) for k in range(groups.bit_length() - 1)]
        rest = [("in", k) for k in range(1, inner.bit_length() - 1)]
        before, after = (rest[:1], rest[1:]) if inner_first else ([], rest)
        self.orders = tuple(before + g + after for g in (grp, grp[:2][::-1] + grp[2:]))
        self.index = {"grp": lax.axis_index("grp"), "in": lax.axis_index("in")}
        self.core = self.index["in"] & 1

    def swap(self, value, stage):
        pairs = []
        for g in range(self.groups):
            for i in range(self.inner):
                axis, bit = ("in", 0) if stage is None else self.orders[i & 1][stage]
                to = (g ^ (1 << bit), i) if axis == "grp" else (g, i ^ (1 << bit))
                pairs.append((g * self.inner + i, to[0] * self.inner + to[1]))
        return lax.ppermute(value, ("grp", "in"), pairs)

    def bit(self, stage):
        bits = [(self.index[axis] >> k) & 1 for axis, k in (order[stage] for order in self.orders)]
        return jnp.where(self.core == 0, bits[0], bits[1])

    def add_halves(self, kept, came):
        orders = self.orders

        def kernel(kept_ref, came_ref, sent_out, kept_out):
            bits = [(lax.axis_index(axis) >> k) & 1 for axis, k in (order[0] for order in orders)]
            bit = jnp.where(lax.axis_index("in") & 1 == 0, bits[0], bits[1])
            part = sent_out.shape[0]
            for out, place in ((sent_out, 1 - bit), (kept_out, bit)):
                rows = pl.ds(pl.multiple_of(place * part, part), part)
                out[...] = kept_ref[rows, :] + came_ref[rows, :]

        half = pltpu.VMEM((kept.shape[0] // 2, kept.shape[1]), F32)
        vmem = pl.BlockSpec(memory_space=pltpu.VMEM)
        return pl.pallas_call(
            kernel,
            in_specs=[vmem] * 2,
            out_specs=[vmem] * 2,
            out_shape=[half] * 2,
            compiler_params=pltpu.CompilerParams(vmem_limit_bytes=8 * 1024 * 1024),
            name="add_halves",
        )(kept, pltpu.with_memory_space_constraint(came, pltpu.VMEM))

    def all_sum(self, sent, kept):
        last = len(self.orders[0]) - 1
        came = self.swap(sent, None)
        if last:
            sent, kept = self.add_halves(kept, came)
            came = self.swap(sent, 0)
        for stage in range(1, last):
            bit = self.bit(stage)
            parts = [x.reshape(2, x.shape[0] // 2, x.shape[1]) for x in (kept, came)]

            def half(place):
                own, new = (lax.dynamic_index_in_dim(x, place, 0, keepdims=False) for x in parts)
                return own + new

            sent, kept = half(1 - bit), half(bit)
            came = self.swap(sent, stage)
        value = kept + came
        value = value + self.swap(value, last)
        for stage in range(last - 1, -1, -1):
            came = self.swap(value, stage)
            bit = self.bit(stage)
            whole = jnp.zeros((2,) + value.shape, value.dtype)
            whole = lax.dynamic_update_index_in_dim(whole, value, bit, 0)
            whole = lax.dynamic_update_index_in_dim(whole, came, 1 - bit, 0)
            value = whole.reshape(-1, value.shape[1])
        return value, self.swap(value, None)


def per_device(groups, inner, unfolding, start_basis):
    parts = gram(unfolding)
    halves = []
    for number in range(len(CHUNKS)):
        exchange = Exchange(groups, inner, number == 0)
        halves += exchange.all_sum(*parts[2 * number : 2 * number + 2])
    factor, core_block = iterate(start_basis, halves, unfolding)
    return (factor, core_block)


def solution(mesh):
    in_specs = (P(None, ("grp", "in")), P())
    out_specs = (P(), P(None, ("grp", "in")))
    body = functools.partial(per_device, mesh.shape["grp"], mesh.shape["in"])
    return jax.shard_map(body, mesh=mesh, in_specs=in_specs, out_specs=out_specs, check_vma=False)
```
